32 devices in a mesh: group: 2 (over x), tensor: 8 (over z, y), dp: 2 (over core).
Axes of the slice: x: 2, y: 2, z: 4, core: 2. Of those that a mesh axis runs over, the one named last changes fastest.
Arguments:
- features: bfloat16 [512, 8192], P(('group', 'dp'), 'tensor'), parts along dimension 0, may hold values from -64 to 64
- cotangent: bfloat16 [512, 8192], P(('group', 'dp'), 'tensor'), parts along dimension 0, may hold values from -64 to 64
- token_tenant: int32 [512], P(('group', 'dp')), parts along dimension 0, may hold values from 0 to 15
- owner_device: int32 [32], P('group'), parts along dimension 0, may hold values from 0 to 15, each once
- frozen_weight: bfloat16 [8192, 8192], P('tensor'), may hold values from -0.09375 to 0.09375
- adapter_down: bfloat16 [32, 16, 8192], P('group', None, 'tensor'), parts along dimension 0, may hold values from -0.0625 to 0.0625
- adapter_up: bfloat16 [32, 16, 8192], P('group', None, 'tensor'), parts along dimension 0, may hold values from -0.29882812 to 0.29882812
- momentum_down: float32 [32, 16, 8192], P(('group', 'tensor', 'dp')), parts along dimension 0, may hold values from -12 to 12
- momentum_up: float32 [32, 16, 8192], P(('group', 'tensor', 'dp')), parts along dimension 0, may hold values from -3 to 3
- variance_down: float32 [32, 16, 8192], P(('group', 'tensor', 'dp')), parts along dimension 0, may hold values from 0.3 to 3
- variance_up: float32 [32, 16, 8192], P(('group', 'tensor', 'dp')), parts along dimension 0, may hold values from 0.02 to 0.2
Outputs:
- projected: bfloat16 [512, 8192], P(('group', 'dp'), 'tensor'), parts along dimension 0
- updated_down: bfloat16 [32, 16, 8192], P('group', None, 'tensor'), parts along dimension 0
- updated_up: bfloat16 [32, 16, 8192], P('group', None, 'tensor'), parts along dimension 0
- mean_down: float32 [32, 16, 8192], P(('group', 'tensor', 'dp')), parts along dimension 0
- mean_up: float32 [32, 16, 8192], P(('group', 'tensor', 'dp')), parts along dimension 0
- power_down: float32 [32, 16, 8192], P(('group', 'tensor', 'dp')), parts along dimension 0
- power_up: float32 [32, 16, 8192], P(('group', 'tensor', 'dp')), parts along dimension 0
The draws below stay inside these ranges and needn't reach their ends.
There are 2 independent parts, one for each index of `group`. The reference program is written for one: setup_inputs(seed, part) draws one part's arguments, and reference() takes and returns one part's arrays. A program takes and returns all parts, laid end to end along the dimension named above; an argument that names none is the same for every part. Nothing has to cross between parts.
Inputs may be any that keep to these rules, and one draw needn't show every extreme that they name: Tenant t belongs to the device whose index along tensor+dp (dp fastest) is owner_device[t]; every index appears once.
All inputs are finite; a program needn't handle non-finite values.
Results may differ from the reference program's by a relative error of at most 0.0014.
The reference program's roundings to bfloat16 on the way count: a program that leaves them out, or rounds other values in their place, can miss the bound.
Values sent between devices are 32-bit elements; how exact they have to be, the bound alone decides.
No kernel may reach another device: no remote copies, remote signals or barrier semaphores. Data moves between devices by JAX's collectives and lax.ppermute only.
A program may use at most 128 MiB of HBM per device.

```python
import math
import jax
import jax.numpy as jnp
import numpy as np
from jax import lax

D = 8192
RANK = 16
TEN = 16
TOKENS = 256


def rough_rows(key, height, breadth):
    subkeys = jax.random.split(key, 3)
    position = jnp.arange(breadth, dtype=jnp.float32) / max(breadth - 1, 1)
    rough_noise = jnp.clip(jax.random.normal(subkeys[0], (height, breadth), jnp.float32), -4.0, 4.0)
    column_trend = jnp.exp(jnp.log(3.0) * position) / 1.7
    row_scale = jnp.exp(jax.random.uniform(subkeys[1], (height, 1), jnp.float32, jnp.log(0.3), jnp.log(3.0)))
    col_scale = column_trend * jnp.exp(jax.random.uniform(subkeys[2], (breadth,), jnp.float32, jnp.log(0.3), jnp.log(3.0)))
    return jnp.clip(rough_noise * row_scale * col_scale[None, :], -64.0, 64.0)


def draw_features(key, part):
    return rough_rows(jax.random.fold_in(key, 11), TOKENS, D).astype(jnp.bfloat16)


def draw_cotangent(key, part):
    return rough_rows(jax.random.fold_in(key, 23), TOKENS, D).astype(jnp.bfloat16)


def set_ends(drawn, stream_key, least, top_value):
    place = [jax.random.randint(jax.random.fold_in(stream_key, axis), (), 0, length) for axis, length in enumerate(drawn.shape)]
    longest = drawn.shape.index(max(drawn.shape))
    neighbour = place[:longest] + [(place[longest] + 1) % drawn.shape[longest]] + place[longest + 1:]
    return drawn.at[tuple(place)].set(least).at[tuple(neighbour)].set(top_value)


def spiked(array, rng, source, target, shards_of, factor):
    def block_of(axis_at):
        return (jnp.arange(array.shape[axis_at]) // (array.shape[axis_at] // shards_of)).reshape((-1,) + (1,) * (array.ndim - 1 - axis_at))

    one_side = jax.random.permutation(rng, shards_of)[block_of(target)]
    other_side = (block_of(target) + shards_of // 2) % shards_of
    return jnp.where((block_of(source) == one_side) | (block_of(source) == other_side), factor * array, array)


def block_levels(key, extent, shards, smallest, largest):
    loudness = 1.0
    for dim, blocks in shards:
        draws = jax.random.uniform(jax.random.fold_in(jax.random.fold_in(key, 6), dim), (blocks,), jnp.float32, smallest / len(shards), largest / len(shards))
        loudness = loudness * jnp.repeat(jnp.exp(draws), extent[dim] // blocks).reshape((-1,) + (1,) * (len(extent) - 1 - dim))
    return loudness


def rank_bounds(number_of, skew):
    loads = [(1 << 20) // math.isqrt(rank ** skew) + 1 for rank in range(1, number_of + 1)]
    scale = 1 + sum(loads) // (1 << 30)
    return np.cumsum(np.array([max(1, weight // scale) for weight in loads]))


def ranked_ids(own_key, shape, count, slope):
    table = rank_bounds(count, slope)
    lot = jax.random.randint(jax.random.fold_in(own_key, 1), shape, 0, int(table[count - 1]))
    grade = jnp.searchsorted(jnp.asarray(table, jnp.int32), lot, side="right")
    return jax.random.permutation(jax.random.fold_in(own_key, 2), count)[grade].astype(jnp.int32)


def scatter_about(stream_key, extent, deviation, bound, cuts=(), held_as=jnp.bfloat16):
    loudness = block_levels(stream_key, extent, cuts, -0.22, 0.18) if cuts else 1.0
    array = jax.random.normal(stream_key, extent, jnp.float32) * deviation * loudness
    return jnp.minimum(jnp.maximum(array, -bound), bound).astype(held_as)


def noise_with(rng, dims, scale, most, pieces, heavy, kind=jnp.bfloat16):
    drawn = scale * jax.random.normal(rng, dims, jnp.float32)
    if pieces:
        drawn = drawn * block_levels(rng, dims, pieces, -0.22, 0.18)
    return jnp.clip(spiked(drawn, jax.random.fold_in(rng, 3), *heavy), -most, most).astype(kind)


def setup_inputs(seed: int = 0, part: int = 0) -> dict:
    splits = jax.random.split(jax.random.key(seed), 12)
    own_keys = jax.random.split(jax.random.fold_in(splits[11], part), 12)
    features = draw_features(jax.random.fold_in(jax.random.fold_in(splits[11], part), 71), part)
    cotangent = draw_cotangent(jax.random.fold_in(jax.random.fold_in(splits[11], part), 71), part)
    token_tenant = set_ends(ranked_ids(own_keys[2], (TOKENS,), TEN, 2), jax.random.fold_in(own_keys[2], 3), 0, TEN - 1).astype(jnp.int32)
    owner_device = jax.random.permutation(own_keys[3], TEN).astype(jnp.int32)
    frozen_weight = noise_with(splits[4], (D, D), D ** -0.5, 0.09375, ((0, 8),), (0, 1, 8, 2.0))
    adapter_down = scatter_about(own_keys[5], (TEN, RANK, D), D ** -0.5, 0.0625, ((2, 8),))
    adapter_up = scatter_about(own_keys[6], (TEN, RANK, D), 0.05, 0.29882812, ((2, 8),))
    momentum_down = scatter_about(own_keys[7], (TEN, RANK, D), 2.0, 12.0, ((0, 16),), jnp.float32)
    momentum_up = scatter_about(own_keys[8], (TEN, RANK, D), 0.5, 3.0, ((0, 16),), jnp.float32)
    variance_down = jnp.clip(jnp.exp(math.log(3.0) - 2.3025851 * jax.random.uniform(own_keys[9], (TEN, RANK, D), jnp.float32) ** block_levels(own_keys[9], (TEN, RANK, D), ((0, 16),), -0.2, 0.2)), 0.3, 3.0)
    variance_up = jnp.clip(jnp.exp(math.log(0.2) - 2.3025851 * jax.random.uniform(own_keys[10], (TEN, RANK, D), jnp.float32) ** block_levels(own_keys[10], (TEN, RANK, D), ((0, 16),), -0.2, 0.2)), 0.02, 0.2)
    return dict(features=features, cotangent=cotangent, token_tenant=token_tenant, owner_device=owner_device, frozen_weight=frozen_weight, adapter_down=adapter_down, adapter_up=adapter_up, momentum_down=momentum_down, momentum_up=momentum_up, variance_down=variance_down, variance_up=variance_up)


adapter_scale = 2.0
clip_norm = 12000.0
learn_rate = 0.004
beta_one = 0.9
beta_two = 0.999
adam_eps = 1e-08
correct_one = 1.0 - beta_one ** 20
correct_two = 1.0 - beta_two ** 20

def tenant_mask(token_tenant, tenants, lowrank):
    columns = lax.broadcasted_iota(jnp.int32, (1, tenants * lowrank), 1) // lowrank
    return token_tenant[:, None] == columns

def rank_fold(tenants, lowrank):
    row_index = lax.broadcasted_iota(jnp.int32, (tenants * lowrank, lowrank), 0) % lowrank
    col_index = lax.broadcasted_iota(jnp.int32, (tenants * lowrank, lowrank), 1)
    return (row_index == col_index).astype(jnp.float32)

def select_rank(scores, token_mask, folding):
    picked = jnp.where(token_mask, scores, jnp.zeros_like(scores))
    return jnp.dot(picked, folding, precision=lax.Precision.HIGHEST, preferred_element_type=jnp.float32)

def spread_rank(values, token_mask, tenants):
    scaled = (adapter_scale * values).astype(jnp.bfloat16)
    tiled_rank = jnp.tile(scaled, (1, tenants))
    return jnp.where(token_mask, tiled_rank, jnp.zeros_like(tiled_rank))

def owner_order(owner_device):
    total = owner_device.shape[0]
    slot_index = lax.broadcasted_iota(jnp.int32, (total, total), 0)
    tenant_index = lax.broadcasted_iota(jnp.int32, (total, total), 1)
    return lax.optimization_barrier(jnp.sum(jnp.where(owner_device[None, :] == slot_index, tenant_index, 0), axis=1)).astype(jnp.int32)

def adam_step(gradient, factor, moment, square):
    clipped = gradient * factor
    moment_next = beta_one * moment + (1.0 - beta_one) * clipped
    square_next = beta_two * square + (1.0 - beta_two) * clipped * clipped
    change = learn_rate * (moment_next / correct_one) / (jnp.sqrt(square_next / correct_two) + adam_eps)
    return (moment_next, square_next, change)

def reference(features, cotangent, token_tenant, owner_device, frozen_weight, adapter_down, adapter_up, momentum_down, momentum_up, variance_down, variance_up):
    tenants, lowrank, width = adapter_down.shape
    token_mask = tenant_mask(token_tenant, tenants, lowrank)
    folding = rank_fold(tenants, lowrank)
    down_flat = adapter_down.reshape(tenants * lowrank, width)
    up_flattened = adapter_up.reshape(tenants * lowrank, width)
    contract = (((1,), (1,)), ((), ()))
    down_sum = select_rank(lax.dot_general(features, down_flat, contract, preferred_element_type=jnp.float32), token_mask, folding)
    up_sum = select_rank(lax.dot_general(cotangent, up_flattened, contract, preferred_element_type=jnp.float32), token_mask, folding)
    frozen_result = jnp.dot(features, frozen_weight, preferred_element_type=jnp.float32)
    down_scattered = spread_rank(down_sum, token_mask, tenants)
    up_scattered = spread_rank(up_sum, token_mask, tenants)
    adapter_result = jnp.dot(down_scattered, up_flattened, preferred_element_type=jnp.float32)
    projected = (frozen_result + adapter_result).astype(jnp.bfloat16)
    outer_product = (((0,), (0,)), ((), ()))
    down_gradient = lax.dot_general(up_scattered, features, outer_product, preferred_element_type=jnp.float32)
    up_gradient = lax.dot_general(down_scattered, cotangent, outer_product, preferred_element_type=jnp.float32)
    down_gradient = down_gradient.reshape(tenants, lowrank, width)
    up_gradient = up_gradient.reshape(tenants, lowrank, width)
    slot_tenant = owner_order(owner_device)
    own_down = jnp.take(down_gradient, slot_tenant, axis=0)
    own_up = jnp.take(up_gradient, slot_tenant, axis=0)
    squares = lax.optimization_barrier(jnp.sum(own_down * own_down, axis=(1, 2))) + lax.optimization_barrier(jnp.sum(own_up * own_up, axis=(1, 2)))
    factor = (clip_norm / jnp.maximum(jnp.sqrt(squares), clip_norm))[:, None, None]
    mean_down, power_down, change_down = adam_step(own_down, factor, momentum_down, variance_down)
    mean_up, power_up, change_up = adam_step(own_up, factor, momentum_up, variance_up)
    back_down = jnp.take(change_down, owner_device, axis=0)
    back_up = jnp.take(change_up, owner_device, axis=0)
    updated_down = (adapter_down.astype(jnp.float32) - back_down).astype(jnp.bfloat16)
    updated_up = (adapter_up.astype(jnp.float32) - back_up).astype(jnp.bfloat16)
    return (projected, updated_down, updated_up, mean_down, mean_up, power_down, power_up)
```

```python
import functools

import jax
import jax.numpy as jnp
from jax import lax
from jax.experimental import pallas as pl
from jax.experimental.pallas import tpu as pltpu
from jax.sharding import PartitionSpec as P

adapter_scale = 2.0
clip_norm = 12000.0
learn_rate = 0.004
beta_one = 0.9
beta_two = 0.999
adam_eps = 1e-08
correct_one = 1.0 - beta_one**20
correct_two = 1.0 - beta_two**20

f32, bf16 = jnp.float32, jnp.bfloat16
vmem = pl.BlockSpec(memory_space=pltpu.VMEM)
smem = pl.BlockSpec(memory_space=pltpu.SMEM)
NT = (((1,), (1,)), ((), ()))
NN = (((1,), (0,)), ((), ()))
TN = (((0,), (0,)), ((), ()))


def params(mib=48):
    return pltpu.CompilerParams(vmem_limit_bytes=mib << 20)


def dot(a, b, dims):
    return lax.dot_general(a, b, dims, preferred_element_type=f32)


def rank_kernel(tenants, lowrank, tenant_ref, feat_ref, cot_ref, down_ref, up_ref, out_ref):
    tokens = feat_ref.shape[0]
    row = lax.broadcasted_iota(jnp.int32, (tenants, lowrank, tokens), 0)
    mine = row == tenant_ref[...].reshape(1, 1, tokens)
    for half, (x_ref, a_ref) in enumerate(((feat_ref, down_ref), (cot_ref, up_ref))):
        scores = dot(a_ref[...], x_ref[...], NT).reshape(tenants, lowrank, tokens)
        out_ref[half * lowrank : (half + 1) * lowrank, :] = jnp.sum(
            jnp.where(mine, scores, 0.0), axis=0
        )


def frozen_kernel(feat_ref, weight_ref, out_ref):
    out_ref[0] = dot(feat_ref[...], weight_ref[...], NN)


def frozen_partials(features, weight, parts):
    tokens, depth = features.shape
    width = weight.shape[1] // parts
    return pl.pallas_call(
        frozen_kernel,
        grid=(parts,),
        in_specs=[
            pl.BlockSpec((tokens, depth), lambda j: (0, 0)),
            pl.BlockSpec((depth, width), lambda j: (0, j)),
        ],
        out_specs=pl.BlockSpec((1, tokens, width), lambda j: (j, 0, 0)),
        out_shape=jax.ShapeDtypeStruct((parts, tokens, width), f32),
        compiler_params=params(),
        cost_estimate=pl.CostEstimate(
            flops=2 * tokens * depth * width * parts,
            bytes_accessed=2 * depth * width * parts + 4 * tokens * width * parts,
            transcendentals=0,
        ),
        name="frozen_partials",
    )(features, weight)


def grad_kernel(
    parts, parts_dp, lowrank, tenants, place_ref, owner_ref, sum_own, sum_other, ten_own, ten_other,
    feat_own, feat_other, cot_own, cot_other, *outs
):
    me, core = place_ref[0], place_ref[1]
    low = jnp.concatenate([sum_own[...], sum_other[...]], axis=1) * adapter_scale
    tenant = jnp.concatenate([ten_own[...], ten_other[...]], axis=1)
    slot = jnp.zeros_like(tenant)
    for t in range(tenants):
        slot = jnp.where(tenant == t, owner_ref[t], slot)
    down, up = low[:lowrank], low[lowrank:]
    picks = [slot == (me ^ k) * parts_dp + core for k in range(parts)]
    for half, (rank, own, other) in enumerate(
        ((up, feat_own, feat_other), (down, cot_own, cot_other))
    ):
        lhs = jnp.concatenate([jnp.where(p, rank, 0.0) for p in picks], axis=0).astype(bf16)
        rhs = jnp.concatenate([own[...], other[...].astype(bf16)], axis=0)
        grad = dot(lhs, rhs, NN)
        for k in range(parts):
            outs[k][half * lowrank : (half + 1) * lowrank, :] = grad[
                k * lowrank : (k + 1) * lowrank
            ]


def adapter_kernel(tenants, lowrank, tenant_ref, sum_ref, up_ref, out_ref):
    low = sum_ref[:lowrank, :] * adapter_scale
    spread = [jnp.where(tenant_ref[...] == t, low, 0.0) for t in range(tenants)]
    lhs = jnp.concatenate(spread, axis=0).astype(bf16)
    out_ref[...] = dot(lhs, up_ref[...], TN)


def adam_kernel(parts, lowrank, width, place_ref, *refs):
    grads = refs[:parts]
    moments, squares = refs[parts : parts + 2], refs[parts + 2 : parts + 4]
    means, powers = refs[parts + 4 : parts + 6], refs[parts + 6 : parts + 8]
    changes = refs[parts + 8 :]
    me = place_ref[0]
    total = jnp.zeros((2 * lowrank, width), f32)
    for ref in grads:
        total = total + ref[...] * ref[...]
    norm = jnp.sqrt(jnp.sum(total, keepdims=True))
    factor = clip_norm / jnp.maximum(norm, clip_norm)
    for k in range(parts):
        columns = pl.ds(pl.multiple_of((me ^ k) * width, width), width)
        for half in range(2):
            rows = pl.ds(half * lowrank, lowrank)
            clipped = grads[k][rows, :] * factor
            mean = beta_one * moments[half][0, :, columns] + (1.0 - beta_one) * clipped
            power = (
                beta_two * squares[half][0, :, columns] + (1.0 - beta_two) * clipped * clipped
            )
            means[half][0, :, columns] = mean
            powers[half][0, :, columns] = power
            changes[k][rows, :] = (
                learn_rate * (mean / correct_one) / (jnp.sqrt(power / correct_two) + adam_eps)
            )


def update_kernel(parts, parts_dp, lowrank, place_ref, slot_ref, down_ref, up_ref, *refs):
    blocks, (down_out, up_out) = refs[: parts * parts_dp], refs[parts * parts_dp :]
    me, core = place_ref[0], place_ref[1]
    for j in range(parts_dp):
        for k in range(parts):
            tenant = slot_ref[(me ^ k) * parts_dp + (core ^ j)]
            block = blocks[j * parts + k]
            down_out[tenant] = (down_ref[tenant].astype(f32) - block[:lowrank]).astype(bf16)
            up_out[tenant] = (up_ref[tenant].astype(f32) - block[lowrank:]).astype(bf16)


def swap(x, axis, bits):
    size = lax.axis_size(axis)
    return lax.ppermute(x, axis, [(i, i ^ bits) for i in range(size)])


def sum_over(x, axis):
    size, low = lax.axis_size(axis), 1
    while low < size:
        reach = 2 if low == 1 else min(4, size // low)
        others = [swap(x, axis, low * j) for j in range(1, reach)]
        for other in others:
            x = x + other
        low *= reach
    return x


def on_device(
    features,
    cotangent,
    token_tenant,
    owner_device,
    frozen_weight,
    adapter_down,
    adapter_up,
    momentum_down,
    momentum_up,
    variance_down,
    variance_up,
):
    tokens = features.shape[0]
    tenants, lowrank, width = adapter_down.shape
    parts = lax.axis_size("tensor")
    parts_dp = lax.axis_size("dp")
    me, core = lax.axis_index("tensor"), lax.axis_index("dp")
    place = jnp.stack([me, core]).astype(jnp.int32)
    tenant_row = token_tenant.reshape(1, tokens)
    down_flat = adapter_down.reshape(tenants * lowrank, width)
    up_flat = adapter_up.reshape(tenants * lowrank, width)
    slot_index = lax.broadcasted_iota(jnp.int32, (tenants, tenants), 0)
    tenant_index = lax.broadcasted_iota(jnp.int32, (tenants, tenants), 1)
    slot_tenant = jnp.sum(jnp.where(owner_device[None, :] == slot_index, tenant_index, 0), axis=1)

    rank_part = pl.pallas_call(
        functools.partial(rank_kernel, tenants, lowrank),
        in_specs=[vmem] * 5,
        out_specs=vmem,
        out_shape=jax.ShapeDtypeStruct((2 * lowrank, tokens), f32),
        compiler_params=params(),
        name="rank_part",
    )(tenant_row, features, cotangent, down_flat, up_flat)
    features_next, cotangent_next, rank_part = lax.optimization_barrier(
        (features, cotangent, rank_part)
    )
    feat_other = swap(features_next.astype(f32), "dp", 1)
    cot_other = swap(cotangent_next.astype(f32), "dp", 1)
    tenant_other = swap(tenant_row, "dp", 1)

    partials = frozen_partials(features_next, frozen_weight, parts)
    frozen_result = lax.psum_scatter(
        partials.reshape(parts * tokens, width), "tensor", scatter_dimension=0, tiled=True
    )

    rank_sum = sum_over(rank_part, "tensor")
    sum_other = swap(rank_sum, "dp", 1)

    grads = pl.pallas_call(
        functools.partial(grad_kernel, parts, parts_dp, lowrank, tenants),
        in_specs=[smem, smem] + [vmem] * 8,
        out_specs=[vmem] * parts,
        out_shape=[jax.ShapeDtypeStruct((2 * lowrank, width), f32)] * parts,
        compiler_params=params(),
        name="gradients",
    )(
        place, owner_device, rank_sum, sum_other, tenant_row, tenant_other,
        features, feat_other, cotangent, cot_other,
    )
    order = sorted(range(1, parts), key=lambda k: (-(k // 2), k))
    got = {0: grads[0]}
    for k in order:
        got[k] = swap(grads[k], "tensor", k)

    adapter_result = pl.pallas_call(
        functools.partial(adapter_kernel, tenants, lowrank),
        in_specs=[vmem] * 3,
        out_specs=vmem,
        out_shape=jax.ShapeDtypeStruct((tokens, width), f32),
        compiler_params=params(),
        name="adapter_result",
    )(tenant_row, rank_sum, up_flat)

    state = jax.ShapeDtypeStruct(momentum_down.shape, f32)
    adam = pl.pallas_call(
        functools.partial(adam_kernel, parts, lowrank, width),
        in_specs=[smem] + [vmem] * (parts + 4),
        out_specs=[vmem] * (parts + 4),
        out_shape=[state] * 4 + [jax.ShapeDtypeStruct((2 * lowrank, width), f32)] * parts,
        compiler_params=params(),
        name="adam",
    )(
        place, *[got[k] for k in range(parts)],
        momentum_down, momentum_up, variance_down, variance_up,
    )
    mean_down, mean_up, power_down, power_up = adam[:4]
    change = adam[4:]
    blocks = {0: change[0]}
    for k in order:
        blocks[k] = swap(change[k], "tensor", k)
    blocks = [blocks[k] for k in range(parts)]
    for k in range(parts):
        blocks.append(swap(blocks[k], "dp", 1))
    updated_down, updated_up = pl.pallas_call(
        functools.partial(update_kernel, parts, parts_dp, lowrank),
        in_specs=[smem, smem] + [vmem] * (2 + parts * parts_dp),
        out_specs=[vmem] * 2,
        out_shape=[jax.ShapeDtypeStruct(adapter_down.shape, bf16)] * 2,
        compiler_params=params(),
        name="update",
    )(place, slot_tenant, adapter_down, adapter_up, *blocks)

    projected = (frozen_result + adapter_result).astype(bf16)
    return (projected, updated_down, updated_up, mean_down, mean_up, power_down, power_up)


def solution(mesh):
    in_specs = (
        P(("group", "dp"), "tensor"),
        P(("group", "dp"), "tensor"),
        P(("group", "dp")),
        P("group"),
        P("tensor", None),
        P("group", None, "tensor"),
        P("group", None, "tensor"),
        P(("group", "tensor", "dp"), None, None),
        P(("group", "tensor", "dp"), None, None),
        P(("group", "tensor", "dp"), None, None),
        P(("group", "tensor", "dp"), None, None),
    )
    out_specs = (
        P(("group", "dp"), "tensor"),
        P("group", None, "tensor"),
        P("group", None, "tensor"),
        P(("group", "tensor", "dp"), None, None),
        P(("group", "tensor", "dp"), None, None),
        P(("group", "tensor", "dp"), None, None),
        P(("group", "tensor", "dp"), None, None),
    )
    return jax.shard_map(
        on_device, mesh=mesh, in_specs=in_specs, out_specs=out_specs, check_vma=False
    )
```

```python
import functools

import jax
import jax.numpy as jnp
from jax import lax
from jax.experimental import pallas as pl
from jax.experimental.pallas import tpu as pltpu
from jax.sharding import PartitionSpec as P

adapter_scale = 2.0
clip_norm = 12000.0
learn_rate = 0.004
beta_one = 0.9
beta_two = 0.999
adam_eps = 1e-08
correct_one = 1.0 - beta_one**20
correct_two = 1.0 - beta_two**20

f32, bf16 = jnp.float32, jnp.bfloat16
vmem = pl.BlockSpec(memory_space=pltpu.VMEM)
smem = pl.BlockSpec(memory_space=pltpu.SMEM)
hbm = pl.BlockSpec(memory_space=pltpu.HBM)
anywhere = pl.BlockSpec(memory_space=pl.ANY)
NT = (((1,), (1,)), ((), ()))
NN = (((1,), (0,)), ((), ()))
TN = (((0,), (0,)), ((), ()))


def params(mib=14):
    return pltpu.CompilerParams(vmem_limit_bytes=mib << 20)


def dot(a, b, dims):
    return lax.dot_general(a, b, dims, preferred_element_type=f32)


hbm_type = type(pltpu.HBM((8,), f32))


def call(body, outs, *args, specs=None, scratch=(), name=None, after=()):
    flat, tree = jax.tree.flatten(outs)
    specs = [vmem] * len(args) if specs is None else list(specs)
    far = [i for i, x in enumerate(args) if isinstance(x, Far)]
    back = [i for i, out in enumerate(flat) if isinstance(out, hbm_type)]
    for i in far:
        specs[i] = hbm
    args = [in_hbm(x.array) if isinstance(x, Far) else x for x in args]
    staged = [pltpu.VMEM(args[i].shape, args[i].dtype) for i in far]
    staged += [pltpu.VMEM(flat[i].shape, flat[i].dtype) for i in back]
    used, extra, count, own = len(args), len(after), len(flat), len(scratch)

    def kernel(*refs):
        ins = list(refs[:used])
        results = list(refs[used + extra : used + extra + count])
        mine = refs[used + extra + count : used + extra + count + own]
        held = refs[used + extra + count + own :]
        loads = [
            pltpu.make_async_copy(ins[i], held[n], held[-1].at[n]) for n, i in enumerate(far)
        ]
        for load in loads:
            load.start()
        for n, i in enumerate(far):
            ins[i] = held[n]
        stores = []
        for n, i in enumerate(back, len(far)):
            stores.append(pltpu.make_async_copy(held[n], results[i], held[-1].at[n]))
            results[i] = held[n]
        for load in loads:
            load.wait()
        body(*ins, *results, *mine)
        for store in stores:
            store.start()
        for store in stores:
            store.wait()

    made = pl.pallas_call(
        kernel,
        in_specs=specs + [anywhere] * extra,
        out_specs=[hbm if isinstance(out, hbm_type) else vmem for out in flat],
        out_shape=flat,
        scratch_shapes=list(scratch) + staged
        + ([pltpu.SemaphoreType.DMA((len(staged),))] if staged else []),
        compiler_params=params(),
        cost_estimate=pl.CostEstimate(flops=0, bytes_accessed=0, transcendentals=0),
        name=name,
    )(*args, *after)
    return jax.tree.unflatten(tree, made)


class Far:
    def __init__(self, array):
        self.array = array


def in_hbm(x):
    return pltpu.with_memory_space_constraint(x, pltpu.HBM)


def rank_kernel(
    tenants, lowrank, tenant_hbm, owner_hbm, feat_hbm, cot_hbm, down_hbm, up_hbm,
    out_ref, rows_ref, ids_ref, tenant_ref, owner_ref, feat_ref, cot_ref, down_ref, up_ref, sems
):
    copies = [
        pltpu.make_async_copy(src, dst, sems.at[i])
        for i, (src, dst) in enumerate(
            (
                (tenant_hbm, tenant_ref), (owner_hbm, owner_ref), (feat_hbm, feat_ref),
                (down_hbm, down_ref), (cot_hbm, cot_ref), (up_hbm, up_ref),
            )
        )
    ]
    for copy in copies:
        copy.start()
    tokens = feat_ref.shape[0]
    row = lax.broadcasted_iota(jnp.int32, (tenants, lowrank, tokens), 0)
    copies[0].wait()
    copies[1].wait()
    tenant = tenant_ref[...]
    slot = jnp.zeros_like(tenant)
    for t in range(tenants):
        slot = jnp.where(tenant == t, owner_ref[:, t : t + 1], slot)
    ids_ref[...] = jnp.zeros_like(ids_ref)
    ids_ref[0:1, :] = tenant.astype(f32)
    ids_ref[1:2, :] = slot.astype(f32)
    out_ref[2 * lowrank :, :] = ids_ref[...]
    mine = row == tenant.reshape(1, 1, tokens)
    for half, (x_ref, a_ref) in enumerate(((feat_ref, down_ref), (cot_ref, up_ref))):
        copies[2 * half + 2].wait()
        copies[2 * half + 3].wait()
        x = x_ref[...]
        scores = dot(a_ref[...].reshape(tenants * lowrank, x.shape[1]), x, NT)
        scores = scores.reshape(tenants, lowrank, tokens)
        out_ref[half * lowrank : (half + 1) * lowrank, :] = jnp.sum(
            jnp.where(mine, scores, 0.0), axis=0
        )
        rows_ref[half * tokens : (half + 1) * tokens, :] = x.astype(f32)


def near_kernel(part, near, across, diagonal, out_ref, ids_ref):
    both = out_ref.shape[0] // 2
    out_ref[:both] = part[:both] + near[:both]
    out_ref[both:] = across[:both] + diagonal[:both]
    ids_ref[...] = across[both:]


def frozen_kernel(ks, first, rows_ref, weight_hbm, out_ref, weight_ref, sems):
    count, tokens, width = out_ref.shape
    whole = weight_hbm.shape[1] // lax.axis_size("tensor")
    me = lax.axis_index("tensor")
    copies = []
    for g, k in enumerate(ks):
        columns = pl.ds(pl.multiple_of((me ^ k) * whole + first, 128), width)
        copies.append(
            pltpu.make_async_copy(
                weight_hbm.at[:, columns],
                weight_ref.at[:, pl.ds(g * width, width)],
                sems.at[g],
            )
        )
        copies[g].start()
    x = rows_ref[:tokens, :].astype(bf16)
    for copy in copies:
        copy.wait()
    result = dot(x, weight_ref[...], NN)
    for g in range(count):
        out_ref[g] = result[:, g * width : (g + 1) * width]


def add_kernel(*refs):
    total = refs[0][...]
    for ref in refs[1:-1]:
        total = total + ref[...]
    refs[-1][...] = total


def merge_kernel(keep_ref, got_ref, send_ref, hold_ref):
    half = send_ref.shape[0]
    send_ref[...] = keep_ref[:half] + got_ref[:half]
    hold_ref[...] = keep_ref[half:] + got_ref[half:]


def finish_kernel(keep_ref, got_ref, out_ref):
    out_ref[...] = keep_ref[0] + got_ref[0]


class Chunk:
    def __init__(self, rows, weight, tokens, parts, first, piece):
        self.bits = [1 << i for i in range(parts.bit_length() - 1)]
        offsets = [0]
        for bit in reversed(self.bits):
            offsets = [k ^ bit for k in offsets] + offsets
        half = parts // 2
        self.merges = len(self.bits) - 1
        self.make = lambda ks, after: call(
            functools.partial(frozen_kernel, ks, first),
            pltpu.HBM((half, tokens, piece), f32), rows, weight,
            specs=[vmem, hbm], name="frozen_blocks", after=after,
            scratch=[
                pltpu.VMEM((weight.shape[0], half * piece), bf16),
                pltpu.SemaphoreType.DMA((half,)),
            ],
        )
        self.halves = offsets[:half], offsets[half:]

    def send(self, *after):
        self.out = self.make(self.halves[0], after)
        self.got = swap(self.out, "tensor", self.bits.pop(0))
        return in_hbm(self.out)

    def keep(self, *after):
        self.hold = self.make(self.halves[1], after)
        return in_hbm(self.hold)

    def merge(self, *after):
        count, tokens, piece = self.hold.shape
        shape = pltpu.HBM((count // 2, tokens, piece), f32)
        self.out, self.hold = call(
            merge_kernel, [shape, shape], Far(self.hold), self.got, after=after, name="merge"
        )
        self.got = swap(self.out, "tensor", self.bits.pop(0))
        self.merges -= 1
        return in_hbm(self.out)

    def finish(self):
        shape = pltpu.HBM(self.hold.shape[1:], f32)
        self.sum = call(finish_kernel, shape, Far(self.hold), self.got, name="finish")
        return in_hbm(self.sum)


def project_kernel(pieces, adapter_ref, *refs):
    out_ref = refs[-1]
    for c, (first, piece) in enumerate(pieces):
        columns = slice(first, first + piece)
        total = refs[c][...] + adapter_ref[:, columns]
        out_ref[:, columns] = total.astype(bf16)


def grad_kernel(parts, sum_ref, ids_own, ids_other, rows_own, rows_other, *outs):
    both, tokens = sum_ref.shape[0] // 2, ids_own.shape[1]
    lowrank = both // 2
    me, core, cores = lax.axis_index("tensor"), lax.axis_index("dp"), lax.axis_size("dp")
    low = jnp.concatenate([sum_ref[:both], sum_ref[both:]], axis=1) * adapter_scale
    slot = jnp.concatenate([ids_own[1:2], ids_other[1:2]], axis=1).astype(jnp.int32)
    picks = [slot == (me ^ k) * cores + core for k in range(parts)]
    for half, rank in enumerate((low[lowrank:], low[:lowrank])):
        these = slice(half * tokens, (half + 1) * tokens)
        lhs = jnp.concatenate([jnp.where(p, rank, 0.0) for p in picks], axis=0).astype(bf16)
        rhs = jnp.concatenate([rows_own[these], rows_other[these]], axis=0).astype(bf16)
        grad = dot(lhs, rhs, NN)
        for k in range(parts):
            outs[k][half * lowrank : (half + 1) * lowrank, :] = grad[
                k * lowrank : (k + 1) * lowrank
            ]


def adapter_kernel(tenants, lowrank, ids_ref, sum_ref, up_ref, out_ref):
    low = sum_ref[:lowrank, :] * adapter_scale
    spread = [jnp.where(ids_ref[0:1].astype(jnp.int32) == t, low, 0.0) for t in range(tenants)]
    lhs = jnp.concatenate(spread, axis=0).astype(bf16)
    out_ref[...] = dot(lhs, up_ref[...], TN)


def clip_factor(grads):
    total = grads[0][...] * grads[0][...]
    for ref in grads[1:]:
        total = total + ref[...] * ref[...]
    return clip_norm / jnp.maximum(jnp.sqrt(jnp.sum(total, keepdims=True)), clip_norm)


def moments_of(grads, state, factor, k, half):
    both, width = grads[k].shape
    lowrank = both // 2
    rows = slice(half * lowrank, (half + 1) * lowrank)
    columns = pl.ds(pl.multiple_of((lax.axis_index("tensor") ^ k) * width, width), width)
    clipped = grads[k][rows, :] * factor
    mean = beta_one * state[half][0, :, columns] + (1.0 - beta_one) * clipped
    power = beta_two * state[2 + half][0, :, columns] + (1.0 - beta_two) * clipped * clipped
    return rows, columns, mean, power


def change_kernel(parts, *refs):
    grads, state, outs = refs[:parts], refs[parts : parts + 4], refs[parts + 4 :]
    factor = clip_factor(grads)
    for k in range(parts):
        for half in range(2):
            rows, _, mean, power = moments_of(grads, state, factor, k, half)
            outs[k][rows, :] = (mean * (learn_rate / correct_one)) / (
                jnp.sqrt(power * (1.0 / correct_two)) + adam_eps
            )


def state_kernel(parts, *refs):
    grads, state = refs[:parts], refs[parts : parts + 4]
    means, powers = refs[parts + 4 : parts + 6], refs[parts + 6 : parts + 8]
    factor = clip_factor(grads)
    for k in range(parts):
        for half in range(2):
            _, columns, mean, power = moments_of(grads, state, factor, k, half)
            means[half][0, :, columns] = mean
            powers[half][0, :, columns] = power


def gate_kernel(x_ref, out_ref):
    out_ref[...] = x_ref[...]


def pack_kernel(*refs):
    for i, ref in enumerate(refs[:-1]):
        refs[-1][i] = ref[...]


def update_kernel(groups, slot_ref, down_ref, up_ref, *refs):
    down_out, up_out = refs[-2:]
    lowrank = down_ref.shape[1]
    me, core, cores = lax.axis_index("tensor"), lax.axis_index("dp"), lax.axis_size("dp")
    for i, ks in enumerate(groups):
        for j in range(2):
            for n, k in enumerate(ks):
                tenant = slot_ref[(me ^ k) * cores + (core ^ j)]
                block = refs[2 * i + j][n]
                down_out[tenant] = (down_ref[tenant].astype(f32) - block[:lowrank]).astype(bf16)
                up_out[tenant] = (up_ref[tenant].astype(f32) - block[lowrank:]).astype(bf16)


def swap(x, axis, bits):
    size = lax.axis_size(axis)
    return lax.ppermute(x, axis, [(i, i ^ bits) for i in range(size)])


def on_device(
    features,
    cotangent,
    token_tenant,
    owner_device,
    frozen_weight,
    adapter_down,
    adapter_up,
    momentum_down,
    momentum_up,
    variance_down,
    variance_up,
):
    tokens = features.shape[0]
    tenants, lowrank, width = adapter_down.shape
    parts = lax.axis_size("tensor")
    parts_dp = lax.axis_size("dp")
    slot_index = lax.broadcasted_iota(jnp.int32, (tenants, tenants), 0)
    tenant_index = lax.broadcasted_iota(jnp.int32, (tenants, tenants), 1)
    slot_tenant = jnp.sum(jnp.where(owner_device[None, :] == slot_index, tenant_index, 0), axis=1)
    bits = [1 << i for i in range(parts.bit_length() - 1)]
    block = jax.ShapeDtypeStruct((2 * lowrank, width), f32)
    low_both = jax.ShapeDtypeStruct((4 * lowrank, tokens), f32)
    id_rows = jax.ShapeDtypeStruct((8, tokens), f32)
    features, cotangent = in_hbm(features), in_hbm(cotangent)
    frozen_weight = in_hbm(frozen_weight)
    state = [Far(x) for x in (momentum_down, momentum_up, variance_down, variance_up)]

    rank_part, rows, ids = call(
        functools.partial(rank_kernel, tenants, lowrank),
        [
            jax.ShapeDtypeStruct((2 * lowrank + 8, tokens), f32),
            jax.ShapeDtypeStruct((2 * tokens, width), f32),
            id_rows,
        ],
        in_hbm(token_tenant.reshape(1, tokens)), in_hbm(owner_device.reshape(1, tenants)),
        features, cotangent, in_hbm(adapter_down), in_hbm(adapter_up),
        specs=[hbm] * 6,
        scratch=[pltpu.VMEM((1, tokens), jnp.int32), pltpu.VMEM((1, tenants), jnp.int32)]
        + [pltpu.VMEM((tokens, width), bf16)] * 2
        + [pltpu.VMEM(adapter_down.shape, bf16)] * 2
        + [pltpu.SemaphoreType.DMA((6,))],
        name="rank_part",
    )
    cores = [(i, i ^ 1) for i in range(parts_dp)]
    diagonal = [
        (t * parts_dp + i, (t ^ 1) * parts_dp + j) for t in range(parts) for i, j in cores
    ]
    rank_sum, ids_other = call(
        near_kernel, [low_both, id_rows], rank_part, swap(rank_part, "tensor", 1),
        swap(rank_part, "dp", 1), lax.ppermute(rank_part, ("tensor", "dp"), diagonal),
        name="rank_near",
    )
    rows_other = swap(rows, "dp", 1)

    units = width // 128
    cuts = sorted({0, (units + 1) // 4 or 1, (5 * units + 4) // 8, units})
    pieces = [(128 * a, 128 * (b - a)) for a, b in zip(cuts, cuts[1:])]
    frozen = [
        Chunk(rows, frozen_weight, tokens, parts, first, piece) for first, piece in pieces
    ]

    sent = frozen[0].send(rank_sum)

    done = 1
    while done < len(bits):
        two = bits[done : done + 2]
        steps = two if len(two) == 1 else [two[0], two[1], two[0] ^ two[1]]
        rank_sum = call(
            add_kernel, low_both, rank_sum, *[swap(rank_sum, "tensor", k) for k in steps],
            name="rank_far", after=[sent],
        )
        done += len(two)

    grads = call(
        functools.partial(grad_kernel, parts), [block] * parts,
        rank_sum, ids, ids_other, rows, rows_other, name="gradients",
    )

    order = sorted(range(2, parts), key=lambda k: (-(k // 2), k))
    order.insert(2, 1)
    flight = 3

    def exchange(made, beside):
        arrived = {0: made[0]}
        for n, k in enumerate(order):
            x = made[k]
            if n >= flight:
                ready = [arrived[j] for j in order[: n - flight + 1]]
                x = call(
                    gate_kernel, block, x, name="gate",
                    after=ready[-1:] + beside(n - flight, ready),
                )
            arrived[k] = swap(x, "tensor", k)
        return arrived

    early, late = frozen[:-1], frozen[-1]
    extra = {}

    def beside_gradients(n, ready):
        if n == 0:
            return [early[0].keep(*ready)]
        if n == 2:
            return [chunk.send(*ready) for chunk in early[1:]]
        if n == 3:
            return [early[0].merge(*ready)] + [chunk.keep(*ready) for chunk in early[1:]]
        return []

    got = exchange(grads, beside_gradients)
    own_grads = [got[k] for k in range(parts)]
    change = call(
        functools.partial(change_kernel, parts), [block] * parts, *own_grads, *state,
        name="change",
    )

    def beside_changes(n, ready):
        if n == 0:
            mine = []
            while early[0].merges:
                mine.append(early[0].merge(*ready))
            return mine
        if n == 1:
            extra["state"] = call(
                functools.partial(state_kernel, parts),
                [pltpu.HBM(momentum_down.shape, f32)] * 4,
                *own_grads, *state, after=ready, name="state",
            )
            return [in_hbm(extra["state"][0])]
        if n == 2:
            return [chunk.merge(*ready) for chunk in early[1:]]
        if n == 3:
            extra["adapter"] = call(
                functools.partial(adapter_kernel, tenants, lowrank),
                jax.ShapeDtypeStruct((tokens, width), f32),
                ids, rank_sum, Far(adapter_up.reshape(tenants * lowrank, width)),
                after=ready, name="adapter_result",
            )
            return [late.send(*ready), late.keep(*ready), extra["adapter"]]
        return []

    back = exchange(change, beside_changes)
    mean_down, mean_up, power_down, power_up = extra["state"]
    adapter_result = extra["adapter"]
    beside = [early[0].finish()]
    for chunk in early[1:]:
        while chunk.merges:
            beside.append(chunk.merge())
    arrive = [0] + order
    groups = [arrive[: parts // 2], arrive[parts // 2 :]]
    sides = []
    for i, ks in enumerate(groups):
        packed = call(
            pack_kernel, jax.ShapeDtypeStruct((len(ks), 2 * lowrank, width), f32),
            *[back[k] for k in ks], name="pack", after=beside if i else [],
        )
        sides += [packed, swap(packed, "dp", 1)]
    updated_down, updated_up = call(
        functools.partial(update_kernel, groups),
        [pltpu.HBM(adapter_down.shape, bf16)] * 2,
        slot_tenant, Far(adapter_down), Far(adapter_up), *sides,
        specs=[smem] + [vmem] * 6,
        name="update",
    )
    for chunk in early[1:]:
        chunk.finish()
    while late.merges:
        late.merge()
    late.finish()
    projected = call(
        functools.partial(project_kernel, pieces),
        pltpu.HBM((tokens, width), bf16),
        Far(adapter_result), *[Far(chunk.sum) for chunk in frozen],
        name="project",
    )
    return (projected, updated_down, updated_up, mean_down, mean_up, power_down, power_up)


def solution(mesh):
    in_specs = (
        P(("group", "dp"), "tensor"),
        P(("group", "dp"), "tensor"),
        P(("group", "dp")),
        P("group"),
        P("tensor", None),
        P("group", None, "tensor"),
        P("group", None, "tensor"),
        P(("group", "tensor", "dp"), None, None),
        P(("group", "tensor", "dp"), None, None),
        P(("group", "tensor", "dp"), None, None),
        P(("group", "tensor", "dp"), None, None),
    )
    out_specs = (
        P(("group", "dp"), "tensor"),
        P("group", None, "tensor"),
        P("group", None, "tensor"),
        P(("group", "tensor", "dp"), None, None),
        P(("group", "tensor", "dp"), None, None),
        P(("group", "tensor", "dp"), None, None),
        P(("group", "tensor", "dp"), None, None),
    )
    return jax.shard_map(
        on_device, mesh=mesh, in_specs=in_specs, out_specs=out_specs, check_vma=False
    )
```

```python
import functools

import jax
import jax.numpy as jnp
from jax import lax
from jax.experimental import pallas as pl
from jax.experimental.pallas import tpu as pltpu
from jax.sharding import PartitionSpec as P

adapter_scale = 2.0
clip_norm = 12000.0
learn_rate = 0.004
beta_one = 0.9
beta_two = 0.999
adam_eps = 1e-08
correct_one = 1.0 - beta_one**20
correct_two = 1.0 - beta_two**20

f32, bf16 = jnp.float32, jnp.bfloat16
vmem = pl.BlockSpec(memory_space=pltpu.VMEM)
smem = pl.BlockSpec(memory_space=pltpu.SMEM)
hbm = pl.BlockSpec(memory_space=pltpu.HBM)
anywhere = pl.BlockSpec(memory_space=pl.ANY)
NT = (((1,), (1,)), ((), ()))
NN = (((1,), (0,)), ((), ()))
TN = (((0,), (0,)), ((), ()))


def params(mib=14):
    return pltpu.CompilerParams(vmem_limit_bytes=mib << 20)


def dot(a, b, dims):
    return lax.dot_general(a, b, dims, preferred_element_type=f32)


hbm_type = type(pltpu.HBM((8,), f32))


def call(body, outs, *args, specs=None, scratch=(), name=None, after=(), stage=True):
    flat, tree = jax.tree.flatten(outs)
    specs = [vmem] * len(args) if specs is None else list(specs)
    far = [i for i, x in enumerate(args) if isinstance(x, Far)]
    back = [i for i, out in enumerate(flat) if stage and isinstance(out, hbm_type)]
    for i in far:
        specs[i] = hbm
    args = [in_hbm(x.array) if isinstance(x, Far) else x for x in args]
    staged = [pltpu.VMEM(args[i].shape, args[i].dtype) for i in far]
    staged += [pltpu.VMEM(flat[i].shape, flat[i].dtype) for i in back]
    used, extra, count, own = len(args), len(after), len(flat), len(scratch)

    def kernel(*refs):
        ins = list(refs[:used])
        results = list(refs[used + extra : used + extra + count])
        mine = refs[used + extra + count : used + extra + count + own]
        held = refs[used + extra + count + own :]
        loads = [
            pltpu.make_async_copy(ins[i], held[n], held[-1].at[n]) for n, i in enumerate(far)
        ]
        for load in loads:
            load.start()
        for n, i in enumerate(far):
            ins[i] = held[n]
        stores = []
        for n, i in enumerate(back, len(far)):
            stores.append(pltpu.make_async_copy(held[n], results[i], held[-1].at[n]))
            results[i] = held[n]
        for load in loads:
            load.wait()
        body(*ins, *results, *mine)
        for store in stores:
            store.start()
        for store in stores:
            store.wait()

    made = pl.pallas_call(
        kernel,
        in_specs=specs + [anywhere] * extra,
        out_specs=[hbm if isinstance(out, hbm_type) else vmem for out in flat],
        out_shape=flat,
        scratch_shapes=list(scratch) + staged
        + ([pltpu.SemaphoreType.DMA((len(staged),))] if staged else []),
        compiler_params=params(),
        cost_estimate=pl.CostEstimate(flops=0, bytes_accessed=0, transcendentals=0),
        name=name,
    )(*args, *after)
    return jax.tree.unflatten(tree, made)


def release(x, after):
    return pl.pallas_call(
        lambda *refs: None,
        in_specs=[anywhere] * (1 + len(after)),
        out_specs=anywhere,
        out_shape=jax.ShapeDtypeStruct(x.shape, x.dtype),
        input_output_aliases={0: 0},
        compiler_params=params(),
        cost_estimate=pl.CostEstimate(flops=0, bytes_accessed=0, transcendentals=0),
        name="release",
    )(x, *after)


class Far:
    def __init__(self, array):
        self.array = array


def in_hbm(x):
    return pltpu.with_memory_space_constraint(x, pltpu.HBM)


def rank_kernel(
    tenants, lowrank, tenant_hbm, owner_hbm, feat_hbm, cot_hbm, down_hbm, up_hbm,
    out_ref, rows_ref, ids_ref, tenant_ref, owner_ref, feat_ref, cot_ref, down_ref, up_ref, sems
):
    copies = [
        pltpu.make_async_copy(src, dst, sems.at[i])
        for i, (src, dst) in enumerate(
            (
                (tenant_hbm, tenant_ref), (owner_hbm, owner_ref), (feat_hbm, feat_ref),
                (down_hbm, down_ref), (cot_hbm, cot_ref), (up_hbm, up_ref),
            )
        )
    ]
    for copy in copies:
        copy.start()
    tokens = feat_ref.shape[0]
    row = lax.broadcasted_iota(jnp.int32, (tenants, lowrank, tokens), 0)
    copies[0].wait()
    copies[1].wait()
    tenant = tenant_ref[...]
    slot = jnp.zeros_like(tenant)
    for t in range(tenants):
        slot = jnp.where(tenant == t, owner_ref[:, t : t + 1], slot)
    ids_ref[...] = jnp.zeros_like(ids_ref)
    ids_ref[0:1, :] = tenant.astype(f32)
    ids_ref[1:2, :] = slot.astype(f32)
    out_ref[2 * lowrank :, :] = ids_ref[...]
    mine = row == tenant.reshape(1, 1, tokens)
    for half, (x_ref, a_ref) in enumerate(((feat_ref, down_ref), (cot_ref, up_ref))):
        copies[2 * half + 2].wait()
        copies[2 * half + 3].wait()
        x = x_ref[...]
        scores = dot(a_ref[...].reshape(tenants * lowrank, x.shape[1]), x, NT)
        scores = scores.reshape(tenants, lowrank, tokens)
        out_ref[half * lowrank : (half + 1) * lowrank, :] = jnp.sum(
            jnp.where(mine, scores, 0.0), axis=0
        )
        rows_ref[half * tokens : (half + 1) * tokens, :] = x.astype(f32)


def near_kernel(part, near, across, diagonal, out_ref, ids_ref):
    both = out_ref.shape[0] // 2
    out_ref[:both] = part[:both] + near[:both]
    out_ref[both:] = across[:both] + diagonal[:both]
    ids_ref[...] = across[both:]


def frozen_kernel(ks, first, rows_ref, weight_hbm, out_hbm, weight_ref, out_ref, sems):
    count, tokens, width = out_ref.shape
    whole = weight_hbm.shape[1] // lax.axis_size("tensor")
    me = lax.axis_index("tensor")
    copies, stores = [], []
    for g, k in enumerate(ks):
        columns = pl.ds(pl.multiple_of((me ^ k) * whole + first, 128), width)
        copies.append(
            pltpu.make_async_copy(
                weight_hbm.at[:, columns],
                weight_ref.at[:, pl.ds(g * width, width)],
                sems.at[g],
            )
        )
        copies[g].start()
    x = rows_ref[:tokens, :].astype(bf16)
    step = max(count // 2, 1)
    for start in range(0, count, step):
        for g in range(start, start + step):
            copies[g].wait()
        result = dot(x, weight_ref[:, start * width : (start + step) * width], NN)
        for g in range(start, start + step):
            out_ref[g] = result[:, (g - start) * width : (g - start + 1) * width]
            stores.append(pltpu.make_async_copy(out_ref.at[g], out_hbm.at[g], sems.at[count + g]))
            stores[g].start()
    for store in stores:
        store.wait()


def add_kernel(*refs):
    total = refs[0][...]
    for ref in refs[1:-1]:
        total = total + ref[...]
    refs[-1][...] = total


def merge_kernel(keep_ref, got_ref, send_ref, hold_ref):
    half = send_ref.shape[0]
    send_ref[...] = keep_ref[:half] + got_ref[:half]
    hold_ref[...] = keep_ref[half:] + got_ref[half:]


class Chunk:
    def __init__(self, rows, weight, tokens, parts, first, piece):
        self.bits = [1 << i for i in range(parts.bit_length() - 1)]
        offsets = [0]
        for bit in reversed(self.bits):
            offsets = [k ^ bit for k in offsets] + offsets
        half = parts // 2
        self.merges = len(self.bits) - 1
        self.make = lambda ks, after: call(
            functools.partial(frozen_kernel, ks, first),
            pltpu.HBM((half, tokens, piece), f32), rows, weight,
            specs=[vmem, hbm], name="frozen_blocks", after=after, stage=False,
            scratch=[
                pltpu.VMEM((weight.shape[0], half * piece), bf16),
                pltpu.VMEM((half, tokens, piece), f32),
                pltpu.SemaphoreType.DMA((2 * half,)),
            ],
        )
        self.halves = offsets[:half], offsets[half:]

    def send(self, *after):
        self.out = self.make(self.halves[0], after)
        return in_hbm(self.out)

    def go(self, *after):
        out = release(self.out, after) if after else self.out
        self.got = swap(out, "tensor", self.bits.pop(0))

    def keep(self, *after):
        self.hold = self.make(self.halves[1], after)
        return in_hbm(self.hold)

    def merge(self, *after):
        count, tokens, piece = self.hold.shape
        shape = pltpu.HBM((count // 2, tokens, piece), f32)
        self.out, self.hold = call(
            merge_kernel, [shape, shape], Far(self.hold), self.got, after=after, name="merge"
        )
        self.got = swap(self.out, "tensor", self.bits.pop(0))
        self.merges -= 1
        return in_hbm(self.out)


def project_kernel(pieces, tenants, ids_ref, sum_ref, up_ref, *refs):
    out_ref = refs[-1]
    lowrank = sum_ref.shape[0] // 4
    low = sum_ref[:lowrank, :] * adapter_scale
    spread = [jnp.where(ids_ref[0:1].astype(jnp.int32) == t, low, 0.0) for t in range(tenants)]
    lhs = jnp.concatenate(spread, axis=0).astype(bf16)
    adapted = dot(lhs, up_ref[...].reshape(tenants * lowrank, up_ref.shape[2]), TN)
    for c, (first, piece) in enumerate(pieces):
        columns = slice(first, first + piece)
        total = refs[2 * c][0] + refs[2 * c + 1][0] + adapted[:, columns]
        out_ref[:, columns] = total.astype(bf16)


def grad_kernel(parts, sum_ref, ids_own, ids_other, rows_own, rows_other, *outs):
    both, tokens = sum_ref.shape[0] // 2, ids_own.shape[1]
    lowrank = both // 2
    me, core, cores = lax.axis_index("tensor"), lax.axis_index("dp"), lax.axis_size("dp")
    low = jnp.concatenate([sum_ref[:both], sum_ref[both:]], axis=1) * adapter_scale
    slot = jnp.concatenate([ids_own[1:2], ids_other[1:2]], axis=1).astype(jnp.int32)
    picks = [slot == (me ^ k) * cores + core for k in range(parts)]
    for half, rank in enumerate((low[lowrank:], low[:lowrank])):
        these = slice(half * tokens, (half + 1) * tokens)
        lhs = jnp.concatenate([jnp.where(p, rank, 0.0) for p in picks], axis=0).astype(bf16)
        rhs = jnp.concatenate([rows_own[these], rows_other[these]], axis=0).astype(bf16)
        grad = dot(lhs, rhs, NN)
        for k in range(parts):
            outs[k][half * lowrank : (half + 1) * lowrank, :] = grad[
                k * lowrank : (k + 1) * lowrank
            ]


def clip_factor(grads):
    total = grads[0][...] * grads[0][...]
    for ref in grads[1:]:
        total = total + ref[...] * ref[...]
    return clip_norm / jnp.maximum(jnp.sqrt(jnp.sum(total, keepdims=True)), clip_norm)


def change_kernel(parts, *refs):
    grads, state, outs = refs[:parts], refs[parts : parts + 4], refs[parts + 4 : 2 * parts + 4]
    state_hbm, sems = refs[2 * parts + 4 : 2 * parts + 8], refs[-1]
    both, width = grads[0].shape
    lowrank = both // 2
    factor = clip_factor(grads)
    places = []
    for k in range(parts):
        columns = pl.ds(pl.multiple_of((lax.axis_index("tensor") ^ k) * width, width), width)
        for half in range(2):
            rows = slice(half * lowrank, (half + 1) * lowrank)
            places.append((k, half, rows, columns))
            clipped = grads[k][rows, :] * factor
            state[half][0, :, columns] = (
                beta_one * state[half][0, :, columns] + (1.0 - beta_one) * clipped
            )
            state[2 + half][0, :, columns] = (
                beta_two * state[2 + half][0, :, columns] + (1.0 - beta_two) * clipped * clipped
            )
    stores = [pltpu.make_async_copy(state[i], state_hbm[i], sems.at[i]) for i in range(4)]
    for store in stores:
        store.start()
    for k, half, rows, columns in places:
        outs[k][rows, :] = (state[half][0, :, columns] * (learn_rate / correct_one)) / (
            jnp.sqrt(state[2 + half][0, :, columns] * (1.0 / correct_two)) + adam_eps
        )
    for store in stores:
        store.wait()


def pack_kernel(*refs):
    for i, ref in enumerate(refs[:-1]):
        refs[-1][i] = ref[...]


def update_kernel(groups, slot_ref, down_ref, up_ref, *refs):
    down_out, up_out = refs[-2:]
    lowrank = down_ref.shape[1]
    me, core, cores = lax.axis_index("tensor"), lax.axis_index("dp"), lax.axis_size("dp")
    for i, ks in enumerate(groups):
        for j in range(2):
            for n, k in enumerate(ks):
                tenant = slot_ref[(me ^ k) * cores + (core ^ j)]
                block = refs[2 * i + j][n]
                down_out[tenant] = (down_ref[tenant].astype(f32) - block[:lowrank]).astype(bf16)
                up_out[tenant] = (up_ref[tenant].astype(f32) - block[lowrank:]).astype(bf16)


def swap(x, axis, bits):
    size = lax.axis_size(axis)
    return lax.ppermute(x, axis, [(i, i ^ bits) for i in range(size)])


def on_device(
    features,
    cotangent,
    token_tenant,
    owner_device,
    frozen_weight,
    adapter_down,
    adapter_up,
    momentum_down,
    momentum_up,
    variance_down,
    variance_up,
):
    tokens = features.shape[0]
    tenants, lowrank, width = adapter_down.shape
    parts = lax.axis_size("tensor")
    parts_dp = lax.axis_size("dp")
    slot_index = lax.broadcasted_iota(jnp.int32, (tenants, tenants), 0)
    tenant_index = lax.broadcasted_iota(jnp.int32, (tenants, tenants), 1)
    slot_tenant = jnp.sum(jnp.where(owner_device[None, :] == slot_index, tenant_index, 0), axis=1)
    bits = [1 << i for i in range(parts.bit_length() - 1)]
    block = jax.ShapeDtypeStruct((2 * lowrank, width), f32)
    low_both = jax.ShapeDtypeStruct((4 * lowrank, tokens), f32)
    id_rows = jax.ShapeDtypeStruct((8, tokens), f32)
    features, cotangent = in_hbm(features), in_hbm(cotangent)
    frozen_weight = in_hbm(frozen_weight)
    state = [Far(x) for x in (momentum_down, momentum_up, variance_down, variance_up)]

    rank_part, rows, ids = call(
        functools.partial(rank_kernel, tenants, lowrank),
        [
            jax.ShapeDtypeStruct((2 * lowrank + 8, tokens), f32),
            jax.ShapeDtypeStruct((2 * tokens, width), f32),
            id_rows,
        ],
        in_hbm(token_tenant.reshape(1, tokens)), in_hbm(owner_device.reshape(1, tenants)),
        features, cotangent, in_hbm(adapter_down), in_hbm(adapter_up),
        specs=[hbm] * 6,
        scratch=[pltpu.VMEM((1, tokens), jnp.int32), pltpu.VMEM((1, tenants), jnp.int32)]
        + [pltpu.VMEM((tokens, width), bf16)] * 2
        + [pltpu.VMEM(adapter_down.shape, bf16)] * 2
        + [pltpu.SemaphoreType.DMA((6,))],
        name="rank_part",
    )
    cores = [(i, i ^ 1) for i in range(parts_dp)]
    diagonal = [
        (t * parts_dp + i, (t ^ 1) * parts_dp + j) for t in range(parts) for i, j in cores
    ]
    rank_sum, ids_other = call(
        near_kernel, [low_both, id_rows], rank_part, swap(rank_part, "tensor", 1),
        swap(rank_part, "dp", 1), lax.ppermute(rank_part, ("tensor", "dp"), diagonal),
        name="rank_near",
    )
    rows_other = swap(rows, "dp", 1)

    units = width // 128
    cuts = sorted({0, (3 * units + 4) // 8 or 1, (6 * units + 4) // 8, units})
    pieces = [(128 * a, 128 * (b - a)) for a, b in zip(cuts, cuts[1:])]
    frozen = [
        Chunk(rows, frozen_weight, tokens, parts, first, piece) for first, piece in pieces
    ]

    sent = frozen[0].send(rank_sum)
    frozen[0].go()

    done = 1
    while done < len(bits):
        two = bits[done : done + 2]
        steps = two if len(two) == 1 else [two[0], two[1], two[0] ^ two[1]]
        rank_sum = call(
            add_kernel, low_both, rank_sum, *[swap(rank_sum, "tensor", k) for k in steps],
            name="rank_far", after=[sent],
        )
        done += len(two)

    grads = call(
        functools.partial(grad_kernel, parts), [block] * parts,
        rank_sum, ids, ids_other, rows, rows_other, name="gradients",
    )

    order = sorted(range(2, parts), key=lambda k: (-(k // 2), k))
    order.insert(2, 1)

    def exchange(made, beside, arrived, flight):
        for n, k in enumerate(order):
            x = made[k]
            if n >= flight:
                ready = [arrived[j] for j in order[: n - flight + 1]]
                x = release(x, ready[-1:] + beside(n - flight, ready))
            arrived[k] = swap(x, "tensor", k)

    early, late = frozen[:-1], frozen[-1]
    second = early[1:]

    def beside_gradients(n, ready):
        if n == 0:
            return [chunk.send(*ready) for chunk in second]
        if n == 1:
            return [early[0].keep(*ready)]
        if n == 2:
            sent = early[0].merge(*ready)
            for chunk in second:
                chunk.go(sent, got[1])
            return [sent]
        return []

    got = {0: grads[0]}
    exchange(grads, beside_gradients, got, 4)
    own_grads = [got[k] for k in range(parts)]
    made = call(
        functools.partial(change_kernel, parts),
        [block] * parts + [pltpu.HBM(momentum_down.shape, f32)] * 4, *own_grads, *state,
        name="change", stage=False, scratch=[pltpu.SemaphoreType.DMA((4,))],
    )
    change, (mean_down, mean_up, power_down, power_up) = made[:parts], made[parts:]

    def beside_changes(n, ready):
        if n == 0:
            return [chunk.keep(*ready) for chunk in second] + [late.send(*ready)]
        if n == 1:
            late.go(back[1], *[chunk.got for chunk in second])
            mine = []
            while early[0].merges:
                mine.append(early[0].merge(*ready))
            return mine
        if n == 2:
            return [chunk.merge(*ready) for chunk in second] + [late.keep(*ready)]
        return []

    back = {0: change[0]}
    exchange(change, beside_changes, back, 4)
    last = back[order[-2]]
    for chunk in second:
        while chunk.merges:
            last = chunk.merge(last)
    late.merge(last, early[0].got, *[back[k] for k in order[3:]])
    while late.merges:
        late.merge(*[chunk.got for chunk in second])
    packed = call(
        pack_kernel, jax.ShapeDtypeStruct((parts, 2 * lowrank, width), f32),
        *[back[k] for k in range(parts)], name="pack", after=[in_hbm(late.out)],
    )
    sides = [packed, swap(packed, "dp", 1)]
    updated_down, updated_up = call(
        functools.partial(update_kernel, [range(parts)]),
        [pltpu.HBM(adapter_down.shape, bf16)] * 2,
        slot_tenant, Far(adapter_down), Far(adapter_up), *sides,
        specs=[smem] + [vmem] * 4,
        name="update",
    )
    projected = call(
        functools.partial(project_kernel, pieces, tenants),
        pltpu.HBM((tokens, width), bf16),
        ids, rank_sum, Far(adapter_up), *[x for chunk in frozen for x in (Far(chunk.hold), chunk.got)],
        name="project", after=[in_hbm(updated_down)],
    )
    return (projected, updated_down, updated_up, mean_down, mean_up, power_down, power_up)


def solution(mesh):
    in_specs = (
        P(("group", "dp"), "tensor"),
        P(("group", "dp"), "tensor"),
        P(("group", "dp")),
        P("group"),
        P("tensor", None),
        P("group", None, "tensor"),
        P("group", None, "tensor"),
        P(("group", "tensor", "dp"), None, None),
        P(("group", "tensor", "dp"), None, None),
        P(("group", "tensor", "dp"), None, None),
        P(("group", "tensor", "dp"), None, None),
    )
    out_specs = (
        P(("group", "dp"), "tensor"),
        P("group", None, "tensor"),
        P("group", None, "tensor"),
        P(("group", "tensor", "dp"), None, None),
        P(("group", "tensor", "dp"), None, None),
        P(("group", "tensor", "dp"), None, None),
        P(("group", "tensor", "dp"), None, None),
    )
    return jax.shard_map(
        on_device, mesh=mesh, in_specs=in_specs, out_specs=out_specs, check_vma=False
    )
```

```python
import functools

import jax
import jax.numpy as jnp
from jax import lax
from jax.experimental import pallas as pl
from jax.experimental.pallas import tpu as pltpu
from jax.sharding import PartitionSpec as P

adapter_scale = 2.0
clip_norm = 12000.0
learn_rate = 0.004
beta_one = 0.9
beta_two = 0.999
adam_eps = 1e-08
correct_one = 1.0 - beta_one**20
correct_two = 1.0 - beta_two**20

f32, bf16 = jnp.float32, jnp.bfloat16
vmem = pl.BlockSpec(memory_space=pltpu.VMEM)
smem = pl.BlockSpec(memory_space=pltpu.SMEM)
hbm = pl.BlockSpec(memory_space=pltpu.HBM)
anywhere = pl.BlockSpec(memory_space=pl.ANY)
NT = (((1,), (1,)), ((), ()))
NN = (((1,), (0,)), ((), ()))
TN = (((0,), (0,)), ((), ()))


def params(mib=14):
    return pltpu.CompilerParams(vmem_limit_bytes=mib << 20)


def dot(a, b, dims):
    return lax.dot_general(a, b, dims, preferred_element_type=f32)


hbm_type = type(pltpu.HBM((8,), f32))


def call(body, outs, *args, specs=None, scratch=(), name=None, after=(), stage=True):
    flat, tree = jax.tree.flatten(outs)
    specs = [vmem] * len(args) if specs is None else list(specs)
    far = [i for i, x in enumerate(args) if isinstance(x, Far)]
    back = [i for i, out in enumerate(flat) if stage and isinstance(out, hbm_type)]
    for i in far:
        specs[i] = hbm
    args = [in_hbm(x.array) if isinstance(x, Far) else x for x in args]
    staged = [pltpu.VMEM(args[i].shape, args[i].dtype) for i in far]
    staged += [pltpu.VMEM(flat[i].shape, flat[i].dtype) for i in back]
    used, extra, count, own = len(args), len(after), len(flat), len(scratch)

    def kernel(*refs):
        ins = list(refs[:used])
        results = list(refs[used + extra : used + extra + count])
        mine = refs[used + extra + count : used + extra + count + own]
        held = refs[used + extra + count + own :]
        loads = [
            pltpu.make_async_copy(ins[i], held[n], held[-1].at[n]) for n, i in enumerate(far)
        ]
        for load in loads:
            load.start()
        for n, i in enumerate(far):
            ins[i] = held[n]
        stores = []
        for n, i in enumerate(back, len(far)):
            stores.append(pltpu.make_async_copy(held[n], results[i], held[-1].at[n]))
            results[i] = held[n]
        for load in loads:
            load.wait()
        body(*ins, *results, *mine)
        for store in stores:
            store.start()
        for store in stores:
            store.wait()

    made = pl.pallas_call(
        kernel,
        in_specs=specs + [anywhere] * extra,
        out_specs=[hbm if isinstance(out, hbm_type) else vmem for out in flat],
        out_shape=flat,
        scratch_shapes=list(scratch) + staged
        + ([pltpu.SemaphoreType.DMA((len(staged),))] if staged else []),
        compiler_params=params(),
        cost_estimate=pl.CostEstimate(flops=0, bytes_accessed=0, transcendentals=0),
        name=name,
    )(*args, *after)
    return jax.tree.unflatten(tree, made)


def release(x, after):
    return pl.pallas_call(
        lambda *refs: None,
        in_specs=[anywhere] * (1 + len(after)),
        out_specs=anywhere,
        out_shape=jax.ShapeDtypeStruct(x.shape, x.dtype),
        input_output_aliases={0: 0},
        compiler_params=params(),
        cost_estimate=pl.CostEstimate(flops=0, bytes_accessed=0, transcendentals=0),
        name="release",
    )(x, *after)


class Far:
    def __init__(self, array):
        self.array = array


def in_hbm(x):
    return pltpu.with_memory_space_constraint(x, pltpu.HBM)


def rank_kernel(
    tenants, lowrank, tenant_hbm, owner_hbm, feat_hbm, cot_hbm, down_hbm, up_hbm,
    out_ref, rows_ref, ids_ref, tenant_ref, owner_ref, feat_ref, cot_ref, down_ref, up_ref, sems
):
    copies = [
        pltpu.make_async_copy(src, dst, sems.at[i])
        for i, (src, dst) in enumerate(
            (
                (tenant_hbm, tenant_ref), (owner_hbm, owner_ref), (feat_hbm, feat_ref),
                (down_hbm, down_ref), (cot_hbm, cot_ref), (up_hbm, up_ref),
            )
        )
    ]
    for copy in copies:
        copy.start()
    tokens = feat_ref.shape[0]
    row = lax.broadcasted_iota(jnp.int32, (tenants, lowrank, tokens), 0)
    copies[0].wait()
    copies[1].wait()
    tenant = tenant_ref[...]
    slot = jnp.zeros_like(tenant)
    for t in range(tenants):
        slot = jnp.where(tenant == t, owner_ref[:, t : t + 1], slot)
    ids_ref[...] = jnp.zeros_like(ids_ref)
    ids_ref[0:1, :] = tenant.astype(f32)
    ids_ref[1:2, :] = slot.astype(f32)
    out_ref[2 * lowrank :, :] = ids_ref[...]
    mine = row == tenant.reshape(1, 1, tokens)
    for half, (x_ref, a_ref) in enumerate(((feat_ref, down_ref), (cot_ref, up_ref))):
        copies[2 * half + 2].wait()
        copies[2 * half + 3].wait()
        x = x_ref[...]
        scores = dot(a_ref[...].reshape(tenants * lowrank, x.shape[1]), x, NT)
        scores = scores.reshape(tenants, lowrank, tokens)
        out_ref[half * lowrank : (half + 1) * lowrank, :] = jnp.sum(
            jnp.where(mine, scores, 0.0), axis=0
        )
        rows_ref[half * tokens : (half + 1) * tokens, :] = x.astype(f32)


def near_kernel(part, near, across, diagonal, out_ref, ids_ref):
    both = out_ref.shape[0] // 2
    out_ref[:both] = part[:both] + near[:both]
    out_ref[both:] = across[:both] + diagonal[:both]
    ids_ref[...] = across[both:]


def frozen_kernel(ks, first, rows_ref, weight_hbm, out_hbm, weight_ref, out_ref, sems):
    count, tokens, width = out_ref.shape
    whole = weight_hbm.shape[1] // lax.axis_size("tensor")
    me = lax.axis_index("tensor")
    copies, stores = [], []
    for g, k in enumerate(ks):
        columns = pl.ds(pl.multiple_of((me ^ k) * whole + first, 128), width)
        copies.append(
            pltpu.make_async_copy(
                weight_hbm.at[:, columns],
                weight_ref.at[:, pl.ds(g * width, width)],
                sems.at[g],
            )
        )
        copies[g].start()
    x = rows_ref[:tokens, :].astype(bf16)
    step = max(count // 2, 1)
    for start in range(0, count, step):
        for g in range(start, start + step):
            copies[g].wait()
        result = dot(x, weight_ref[:, start * width : (start + step) * width], NN)
        for g in range(start, start + step):
            out_ref[g] = result[:, (g - start) * width : (g - start + 1) * width]
            stores.append(pltpu.make_async_copy(out_ref.at[g], out_hbm.at[g], sems.at[count + g]))
            stores[g].start()
    for store in stores:
        store.wait()


def add_kernel(*refs):
    total = refs[0][...]
    for ref in refs[1:-1]:
        total = total + ref[...]
    refs[-1][...] = total


def merge_kernel(keep_ref, got_ref, send_ref, hold_ref):
    half = send_ref.shape[0]
    send_ref[...] = keep_ref[:half] + got_ref[:half]
    hold_ref[...] = keep_ref[half:] + got_ref[half:]


class Chunk:
    def __init__(self, rows, weight, tokens, parts, first, piece):
        self.bits = [1 << i for i in range(parts.bit_length() - 1)]
        offsets = [0]
        for bit in reversed(self.bits):
            offsets = [k ^ bit for k in offsets] + offsets
        half = parts // 2
        self.merges = len(self.bits) - 1
        self.make = lambda ks, after: call(
            functools.partial(frozen_kernel, ks, first),
            pltpu.HBM((half, tokens, piece), f32), rows, weight,
            specs=[vmem, hbm], name="frozen_blocks", after=after, stage=False,
            scratch=[
                pltpu.VMEM((weight.shape[0], half * piece), bf16),
                pltpu.VMEM((half, tokens, piece), f32),
                pltpu.SemaphoreType.DMA((2 * half,)),
            ],
        )
        self.halves = offsets[:half], offsets[half:]

    def send(self, *after):
        self.out = self.make(self.halves[0], after)
        return in_hbm(self.out)

    def go(self, *after):
        out = release(self.out, after) if after else self.out
        self.got = swap(out, "tensor", self.bits.pop(0))

    def keep(self, *after):
        self.hold = self.make(self.halves[1], after)
        return in_hbm(self.hold)

    def merge(self, *after):
        count, tokens, piece = self.hold.shape
        shape = pltpu.HBM((count // 2, tokens, piece), f32)
        self.out, self.hold = call(
            merge_kernel, [shape, shape], Far(self.hold), self.got, after=after, name="merge"
        )
        self.got = swap(self.out, "tensor", self.bits.pop(0))
        self.merges -= 1
        return in_hbm(self.out)


def project_kernel(pieces, tenants, ids_ref, sum_ref, up_ref, *refs):
    out_ref = refs[-1]
    lowrank = sum_ref.shape[0] // 4
    low = sum_ref[:lowrank, :] * adapter_scale
    spread = [jnp.where(ids_ref[0:1].astype(jnp.int32) == t, low, 0.0) for t in range(tenants)]
    lhs = jnp.concatenate(spread, axis=0).astype(bf16)
    adapted = dot(lhs, up_ref[...].reshape(tenants * lowrank, up_ref.shape[2]), TN)
    for c, (first, piece) in enumerate(pieces):
        columns = slice(first, first + piece)
        total = refs[2 * c][0] + refs[2 * c + 1][0] + adapted[:, columns]
        out_ref[:, columns] = total.astype(bf16)


def grad_kernel(parts, sum_ref, ids_own, ids_other, rows_own, rows_other, *outs):
    both, tokens = sum_ref.shape[0] // 2, ids_own.shape[1]
    lowrank = both // 2
    me, core, cores = lax.axis_index("tensor"), lax.axis_index("dp"), lax.axis_size("dp")
    low = jnp.concatenate([sum_ref[:both], sum_ref[both:]], axis=1) * adapter_scale
    slot = jnp.concatenate([ids_own[1:2], ids_other[1:2]], axis=1).astype(jnp.int32)
    picks = [slot == (me ^ k) * cores + core for k in range(parts)]
    for half, rank in enumerate((low[lowrank:], low[:lowrank])):
        these = slice(half * tokens, (half + 1) * tokens)
        lhs = jnp.concatenate([jnp.where(p, rank, 0.0) for p in picks], axis=0).astype(bf16)
        rhs = jnp.concatenate([rows_own[these], rows_other[these]], axis=0).astype(bf16)
        grad = dot(lhs, rhs, NN)
        for k in range(parts):
            outs[k][half * lowrank : (half + 1) * lowrank, :] = grad[
                k * lowrank : (k + 1) * lowrank
            ]


def clip_factor(grads):
    total = grads[0][...] * grads[0][...]
    for ref in grads[1:]:
        total = total + ref[...] * ref[...]
    return clip_norm / jnp.maximum(jnp.sqrt(jnp.sum(total, keepdims=True)), clip_norm)


def change_kernel(parts, *refs):
    grads, state, outs = refs[:parts], refs[parts : parts + 4], refs[parts + 4 : 2 * parts + 4]
    state_hbm, sems = refs[2 * parts + 4 : 2 * parts + 8], refs[-1]
    both, width = grads[0].shape
    lowrank = both // 2
    factor = clip_factor(grads)
    places = []
    for k in range(parts):
        columns = pl.ds(pl.multiple_of((lax.axis_index("tensor") ^ k) * width, width), width)
        for half in range(2):
            rows = slice(half * lowrank, (half + 1) * lowrank)
            places.append((k, half, rows, columns))
            clipped = grads[k][rows, :] * factor
            state[half][0, :, columns] = (
                beta_one * state[half][0, :, columns] + (1.0 - beta_one) * clipped
            )
            state[2 + half][0, :, columns] = (
                beta_two * state[2 + half][0, :, columns] + (1.0 - beta_two) * clipped * clipped
            )
    stores = [pltpu.make_async_copy(state[i], state_hbm[i], sems.at[i]) for i in range(4)]
    for store in stores:
        store.start()
    for k, half, rows, columns in places:
        outs[k][rows, :] = (state[half][0, :, columns] * (learn_rate / correct_one)) / (
            jnp.sqrt(state[2 + half][0, :, columns] * (1.0 / correct_two)) + adam_eps
        )
    for store in stores:
        store.wait()


def pack_kernel(*refs):
    for i, ref in enumerate(refs[:-1]):
        refs[-1][i] = ref[...]


def update_kernel(groups, slot_ref, down_ref, up_ref, *refs):
    down_out, up_out = refs[-2:]
    lowrank = down_ref.shape[1]
    me, core, cores = lax.axis_index("tensor"), lax.axis_index("dp"), lax.axis_size("dp")
    for i, ks in enumerate(groups):
        for j in range(2):
            for n, k in enumerate(ks):
                tenant = slot_ref[(me ^ k) * cores + (core ^ j)]
                block = refs[2 * i + j][n]
                down_out[tenant] = (down_ref[tenant].astype(f32) - block[:lowrank]).astype(bf16)
                up_out[tenant] = (up_ref[tenant].astype(f32) - block[lowrank:]).astype(bf16)


def swap(x, axis, bits):
    size = lax.axis_size(axis)
    return lax.ppermute(x, axis, [(i, i ^ bits) for i in range(size)])


def on_device(
    features,
    cotangent,
    token_tenant,
    owner_device,
    frozen_weight,
    adapter_down,
    adapter_up,
    momentum_down,
    momentum_up,
    variance_down,
    variance_up,
):
    tokens = features.shape[0]
    tenants, lowrank, width = adapter_down.shape
    parts = lax.axis_size("tensor")
    parts_dp = lax.axis_size("dp")
    slot_index = lax.broadcasted_iota(jnp.int32, (tenants, tenants), 0)
    tenant_index = lax.broadcasted_iota(jnp.int32, (tenants, tenants), 1)
    slot_tenant = jnp.sum(jnp.where(owner_device[None, :] == slot_index, tenant_index, 0), axis=1)
    bits = [1 << i for i in range(parts.bit_length() - 1)]
    block = jax.ShapeDtypeStruct((2 * lowrank, width), f32)
    low_both = jax.ShapeDtypeStruct((4 * lowrank, tokens), f32)
    id_rows = jax.ShapeDtypeStruct((8, tokens), f32)
    features, cotangent = in_hbm(features), in_hbm(cotangent)
    frozen_weight = in_hbm(frozen_weight)
    state = [Far(x) for x in (momentum_down, momentum_up, variance_down, variance_up)]

    rank_part, rows, ids = call(
        functools.partial(rank_kernel, tenants, lowrank),
        [
            jax.ShapeDtypeStruct((2 * lowrank + 8, tokens), f32),
            jax.ShapeDtypeStruct((2 * tokens, width), f32),
            id_rows,
        ],
        in_hbm(token_tenant.reshape(1, tokens)), in_hbm(owner_device.reshape(1, tenants)),
        features, cotangent, in_hbm(adapter_down), in_hbm(adapter_up),
        specs=[hbm] * 6,
        scratch=[pltpu.VMEM((1, tokens), jnp.int32), pltpu.VMEM((1, tenants), jnp.int32)]
        + [pltpu.VMEM((tokens, width), bf16)] * 2
        + [pltpu.VMEM(adapter_down.shape, bf16)] * 2
        + [pltpu.SemaphoreType.DMA((6,))],
        name="rank_part",
    )
    cores = [(i, i ^ 1) for i in range(parts_dp)]
    diagonal = [
        (t * parts_dp + i, (t ^ 1) * parts_dp + j) for t in range(parts) for i, j in cores
    ]
    rank_sum, ids_other = call(
        near_kernel, [low_both, id_rows], rank_part, swap(rank_part, "tensor", 1),
        swap(rank_part, "dp", 1), lax.ppermute(rank_part, ("tensor", "dp"), diagonal),
        name="rank_near",
    )
    rows_other = swap(rows, "dp", 1)

    units = width // 128
    cuts = sorted({0, (3 * units + 4) // 8 or 1, (6 * units + 4) // 8, units})
    pieces = [(128 * a, 128 * (b - a)) for a, b in zip(cuts, cuts[1:])]
    frozen = [
        Chunk(rows, frozen_weight, tokens, parts, first, piece) for first, piece in pieces
    ]

    sent = frozen[0].send(rank_sum)
    frozen[0].go()

    done = 1
    while done < len(bits):
        two = bits[done : done + 2]
        steps = two if len(two) == 1 else [two[0], two[1], two[0] ^ two[1]]
        rank_sum = call(
            add_kernel, low_both, rank_sum, *[swap(rank_sum, "tensor", k) for k in steps],
            name="rank_far", after=[sent],
        )
        done += len(two)

    grads = call(
        functools.partial(grad_kernel, parts), [block] * parts,
        rank_sum, ids, ids_other, rows, rows_other, name="gradients",
    )

    order = sorted(range(2, parts), key=lambda k: (-(k // 2), k))
    order.insert(2, 1)

    def exchange(made, beside, arrived, flight):
        for n, k in enumerate(order):
            x = made[k]
            if n >= flight:
                ready = [arrived[j] for j in order[: n - flight + 1]]
                x = release(x, ready[-1:] + beside(n - flight, ready))
            arrived[k] = swap(x, "tensor", k)

    early, late = frozen[:-1], frozen[-1]
    second = early[1:]

    def beside_gradients(n, ready):
        if n == 0:
            return [early[0].keep(*ready)]
        if n == 1:
            return [chunk.send(*ready) for chunk in second]
        if n == 2:
            sent = early[0].merge(*ready)
            for chunk in second:
                chunk.go(sent, got[1])
            return [sent]
        return []

    got = {0: grads[0]}
    exchange(grads, beside_gradients, got, 4)
    own_grads = [got[k] for k in range(parts)]
    made = call(
        functools.partial(change_kernel, parts),
        [block] * parts + [pltpu.HBM(momentum_down.shape, f32)] * 4, *own_grads, *state,
        name="change", stage=False, scratch=[pltpu.SemaphoreType.DMA((4,))],
    )
    change, (mean_down, mean_up, power_down, power_up) = made[:parts], made[parts:]

    def beside_changes(n, ready):
        if n == 0:
            return [chunk.keep(*ready) for chunk in second] + [late.send(*ready)]
        if n == 1:
            late.go(back[1], *[chunk.got for chunk in second])
            return []
        if n == 2:
            mine = [chunk.merge(*ready) for chunk in second]
            while early[0].merges:
                mine.append(early[0].merge(*mine))
            return mine + [late.keep(*mine)]
        return []

    back = {0: change[0]}
    exchange(change, beside_changes, back, 4)
    last = back[order[-2]]
    for chunk in second:
        while chunk.merges:
            last = chunk.merge(last)
    late.merge(last, early[0].got, *[back[k] for k in order[3:]])
    while late.merges:
        late.merge(*[chunk.got for chunk in second])
    packed = call(
        pack_kernel, jax.ShapeDtypeStruct((parts, 2 * lowrank, width), f32),
        *[back[k] for k in range(parts)], name="pack", after=[in_hbm(late.out)],
    )
    sides = [packed, swap(packed, "dp", 1)]
    updated_down, updated_up = call(
        functools.partial(update_kernel, [range(parts)]),
        [pltpu.HBM(adapter_down.shape, bf16)] * 2,
        slot_tenant, Far(adapter_down), Far(adapter_up), *sides,
        specs=[smem] + [vmem] * 4,
        name="update",
    )
    projected = call(
        functools.partial(project_kernel, pieces, tenants),
        pltpu.HBM((tokens, width), bf16),
        ids, rank_sum, Far(adapter_up), *[x for chunk in frozen for x in (Far(chunk.hold), chunk.got)],
        name="project", after=[in_hbm(updated_down)],
    )
    return (projected, updated_down, updated_up, mean_down, mean_up, power_down, power_up)


def solution(mesh):
    in_specs = (
        P(("group", "dp"), "tensor"),
        P(("group", "dp"), "tensor"),
        P(("group", "dp")),
        P("group"),
        P("tensor", None),
        P("group", None, "tensor"),
        P("group", None, "tensor"),
        P(("group", "tensor", "dp"), None, None),
        P(("group", "tensor", "dp"), None, None),
        P(("group", "tensor", "dp"), None, None),
        P(("group", "tensor", "dp"), None, None),
    )
    out_specs = (
        P(("group", "dp"), "tensor"),
        P("group", None, "tensor"),
        P("group", None, "tensor"),
        P(("group", "tensor", "dp"), None, None),
        P(("group", "tensor", "dp"), None, None),
        P(("group", "tensor", "dp"), None, None),
        P(("group", "tensor", "dp"), None, None),
    )
    return jax.shard_map(
        on_device, mesh=mesh, in_specs=in_specs, out_specs=out_specs, check_vma=False
    )
```

```python
import functools

import jax
import jax.numpy as jnp
from jax import lax
from jax.experimental import pallas as pl
from jax.experimental.pallas import tpu as pltpu
from jax.sharding import PartitionSpec as P

adapter_scale = 2.0
clip_norm = 12000.0
learn_rate = 0.004
beta_one = 0.9
beta_two = 0.999
adam_eps = 1e-08
correct_one = 1.0 - beta_one**20
correct_two = 1.0 - beta_two**20

f32, bf16 = jnp.float32, jnp.bfloat16
vmem = pl.BlockSpec(memory_space=pltpu.VMEM)
smem = pl.BlockSpec(memory_space=pltpu.SMEM)
hbm = pl.BlockSpec(memory_space=pltpu.HBM)
anywhere = pl.BlockSpec(memory_space=pl.ANY)
NT = (((1,), (1,)), ((), ()))
NN = (((1,), (0,)), ((), ()))
TN = (((0,), (0,)), ((), ()))


def params(mib=14):
    return pltpu.CompilerParams(vmem_limit_bytes=mib << 20)


def dot(a, b, dims):
    return lax.dot_general(a, b, dims, preferred_element_type=f32)


hbm_type = type(pltpu.HBM((8,), f32))


def call(body, outs, *args, specs=None, scratch=(), name=None, after=(), stage=True):
    flat, tree = jax.tree.flatten(outs)
    specs = [vmem] * len(args) if specs is None else list(specs)
    far = [i for i, x in enumerate(args) if isinstance(x, Far)]
    back = [i for i, out in enumerate(flat) if stage and isinstance(out, hbm_type)]
    for i in far:
        specs[i] = hbm
    args = [in_hbm(x.array) if isinstance(x, Far) else x for x in args]
    staged = [pltpu.VMEM(args[i].shape, args[i].dtype) for i in far]
    staged += [pltpu.VMEM(flat[i].shape, flat[i].dtype) for i in back]
    used, extra, count, own = len(args), len(after), len(flat), len(scratch)

    def kernel(*refs):
        ins = list(refs[:used])
        results = list(refs[used + extra : used + extra + count])
        mine = refs[used + extra + count : used + extra + count + own]
        held = refs[used + extra + count + own :]
        loads = [
            pltpu.make_async_copy(ins[i], held[n], held[-1].at[n]) for n, i in enumerate(far)
        ]
        for load in loads:
            load.start()
        for n, i in enumerate(far):
            ins[i] = held[n]
        stores = []
        for n, i in enumerate(back, len(far)):
            stores.append(pltpu.make_async_copy(held[n], results[i], held[-1].at[n]))
            results[i] = held[n]
        for load in loads:
            load.wait()
        body(*ins, *results, *mine)
        for store in stores:
            store.start()
        for store in stores:
            store.wait()

    made = pl.pallas_call(
        kernel,
        in_specs=specs + [anywhere] * extra,
        out_specs=[hbm if isinstance(out, hbm_type) else vmem for out in flat],
        out_shape=flat,
        scratch_shapes=list(scratch) + staged
        + ([pltpu.SemaphoreType.DMA((len(staged),))] if staged else []),
        compiler_params=params(),
        cost_estimate=pl.CostEstimate(flops=0, bytes_accessed=0, transcendentals=0),
        name=name,
    )(*args, *after)
    return jax.tree.unflatten(tree, made)


def release(x, after):
    return pl.pallas_call(
        lambda *refs: None,
        in_specs=[anywhere] * (1 + len(after)),
        out_specs=anywhere,
        out_shape=jax.ShapeDtypeStruct(x.shape, x.dtype),
        input_output_aliases={0: 0},
        compiler_params=params(),
        cost_estimate=pl.CostEstimate(flops=0, bytes_accessed=0, transcendentals=0),
        name="release",
    )(x, *after)


class Far:
    def __init__(self, array):
        self.array = array


def in_hbm(x):
    return pltpu.with_memory_space_constraint(x, pltpu.HBM)


def rank_kernel(
    tenants, lowrank, tenant_hbm, owner_hbm, feat_hbm, cot_hbm, down_hbm, up_hbm,
    out_ref, rows_ref, ids_ref, tenant_ref, owner_ref, feat_ref, cot_ref, down_ref, up_ref, sems
):
    copies = [
        pltpu.make_async_copy(src, dst, sems.at[i])
        for i, (src, dst) in enumerate(
            (
                (tenant_hbm, tenant_ref), (owner_hbm, owner_ref), (feat_hbm, feat_ref),
                (down_hbm, down_ref), (cot_hbm, cot_ref), (up_hbm, up_ref),
            )
        )
    ]
    for copy in copies:
        copy.start()
    tokens = feat_ref.shape[0]
    row = lax.broadcasted_iota(jnp.int32, (tenants, lowrank, tokens), 0)
    copies[0].wait()
    copies[1].wait()
    tenant = tenant_ref[...]
    slot = jnp.zeros_like(tenant)
    for t in range(tenants):
        slot = jnp.where(tenant == t, owner_ref[:, t : t + 1], slot)
    ids_ref[...] = jnp.zeros_like(ids_ref)
    ids_ref[0:1, :] = tenant.astype(f32)
    ids_ref[1:2, :] = slot.astype(f32)
    out_ref[2 * lowrank :, :] = ids_ref[...]
    mine = row == tenant.reshape(1, 1, tokens)
    for half, (x_ref, a_ref) in enumerate(((feat_ref, down_ref), (cot_ref, up_ref))):
        copies[2 * half + 2].wait()
        copies[2 * half + 3].wait()
        x = x_ref[...]
        scores = dot(a_ref[...].reshape(tenants * lowrank, x.shape[1]), x, NT)
        scores = scores.reshape(tenants, lowrank, tokens)
        out_ref[half * lowrank : (half + 1) * lowrank, :] = jnp.sum(
            jnp.where(mine, scores, 0.0), axis=0
        )
        rows_ref[half * tokens : (half + 1) * tokens, :] = x.astype(f32)


def near_kernel(part, near, across, diagonal, out_ref, ids_ref):
    both = out_ref.shape[0] // 2
    out_ref[:both] = part[:both] + near[:both]
    out_ref[both:] = across[:both] + diagonal[:both]
    ids_ref[...] = across[both:]


def frozen_kernel(ks, first, rows_ref, weight_hbm, out_hbm, weight_ref, out_ref, sems):
    count, tokens, width = out_ref.shape
    whole = weight_hbm.shape[1] // lax.axis_size("tensor")
    me = lax.axis_index("tensor")
    copies, stores = [], []
    for g, k in enumerate(ks):
        columns = pl.ds(pl.multiple_of((me ^ k) * whole + first, 128), width)
        copies.append(
            pltpu.make_async_copy(
                weight_hbm.at[:, columns],
                weight_ref.at[:, pl.ds(g * width, width)],
                sems.at[g],
            )
        )
        copies[g].start()
    x = rows_ref[:tokens, :].astype(bf16)
    step = max(count // 2, 1)
    for start in range(0, count, step):
        for g in range(start, start + step):
            copies[g].wait()
        result = dot(x, weight_ref[:, start * width : (start + step) * width], NN)
        for g in range(start, start + step):
            out_ref[g] = result[:, (g - start) * width : (g - start + 1) * width]
            stores.append(pltpu.make_async_copy(out_ref.at[g], out_hbm.at[g], sems.at[count + g]))
            stores[g].start()
    for store in stores:
        store.wait()


def add_kernel(*refs):
    total = refs[0][...]
    for ref in refs[1:-1]:
        total = total + ref[...]
    refs[-1][...] = total


def merge_kernel(keep_ref, got_ref, send_ref, hold_ref):
    half = send_ref.shape[0]
    send_ref[...] = keep_ref[:half] + got_ref[:half]
    hold_ref[...] = keep_ref[half:] + got_ref[half:]


class Chunk:
    def __init__(self, rows, weight, tokens, parts, first, piece):
        self.bits = [1 << i for i in range(parts.bit_length() - 1)]
        offsets = [0]
        for bit in reversed(self.bits):
            offsets = [k ^ bit for k in offsets] + offsets
        half = parts // 2
        self.merges = len(self.bits) - 1
        self.make = lambda ks, after: call(
            functools.partial(frozen_kernel, ks, first),
            pltpu.HBM((half, tokens, piece), f32), rows, weight,
            specs=[vmem, hbm], name="frozen_blocks", after=after, stage=False,
            scratch=[
                pltpu.VMEM((weight.shape[0], half * piece), bf16),
                pltpu.VMEM((half, tokens, piece), f32),
                pltpu.SemaphoreType.DMA((2 * half,)),
            ],
        )
        self.halves = offsets[:half], offsets[half:]

    def send(self, *after):
        self.out = self.make(self.halves[0], after)
        return in_hbm(self.out)

    def go(self, *after):
        out = release(self.out, after) if after else self.out
        self.got = swap(out, "tensor", self.bits.pop(0))

    def keep(self, *after):
        self.hold = self.make(self.halves[1], after)
        return in_hbm(self.hold)

    def merge(self, *after):
        count, tokens, piece = self.hold.shape
        shape = pltpu.HBM((count // 2, tokens, piece), f32)
        self.out, self.hold = call(
            merge_kernel, [shape, shape], Far(self.hold), self.got, after=after, name="merge"
        )
        self.got = swap(self.out, "tensor", self.bits.pop(0))
        self.merges -= 1
        return in_hbm(self.out)


def project_kernel(pieces, tenants, ids_ref, sum_ref, up_ref, *refs):
    out_ref = refs[-1]
    lowrank = sum_ref.shape[0] // 4
    low = sum_ref[:lowrank, :] * adapter_scale
    spread = [jnp.where(ids_ref[0:1].astype(jnp.int32) == t, low, 0.0) for t in range(tenants)]
    lhs = jnp.concatenate(spread, axis=0).astype(bf16)
    adapted = dot(lhs, up_ref[...].reshape(tenants * lowrank, up_ref.shape[2]), TN)
    for c, (first, piece) in enumerate(pieces):
        columns = slice(first, first + piece)
        total = refs[2 * c][0] + refs[2 * c + 1][0] + adapted[:, columns]
        out_ref[:, columns] = total.astype(bf16)


def grad_kernel(parts, sum_ref, ids_own, ids_other, rows_own, rows_other, *outs):
    both, tokens = sum_ref.shape[0] // 2, ids_own.shape[1]
    lowrank = both // 2
    me, core, cores = lax.axis_index("tensor"), lax.axis_index("dp"), lax.axis_size("dp")
    low = jnp.concatenate([sum_ref[:both], sum_ref[both:]], axis=1) * adapter_scale
    slot = jnp.concatenate([ids_own[1:2], ids_other[1:2]], axis=1).astype(jnp.int32)
    picks = [slot == (me ^ k) * cores + core for k in range(parts)]
    for half, rank in enumerate((low[lowrank:], low[:lowrank])):
        these = slice(half * tokens, (half + 1) * tokens)
        lhs = jnp.concatenate([jnp.where(p, rank, 0.0) for p in picks], axis=0).astype(bf16)
        rhs = jnp.concatenate([rows_own[these], rows_other[these]], axis=0).astype(bf16)
        grad = dot(lhs, rhs, NN)
        for k in range(parts):
            outs[k][half * lowrank : (half + 1) * lowrank, :] = grad[
                k * lowrank : (k + 1) * lowrank
            ]


def clip_factor(grads):
    total = grads[0][...] * grads[0][...]
    for ref in grads[1:]:
        total = total + ref[...] * ref[...]
    return clip_norm / jnp.maximum(jnp.sqrt(jnp.sum(total, keepdims=True)), clip_norm)


def change_kernel(parts, *refs):
    grads, state_in, outs = refs[:parts], refs[parts : parts + 4], refs[parts + 4 : 2 * parts + 4]
    state_out, state, sems = refs[2 * parts + 4 : 2 * parts + 8], refs[-5:-1], refs[-1]
    loads = [pltpu.make_async_copy(state_in[i], state[i], sems.at[4 + i]) for i in range(4)]
    stores = [pltpu.make_async_copy(state[i], state_out[i], sems.at[i]) for i in range(4)]
    for i in (0, 2, 1, 3):
        loads[i].start()
    both, width = grads[0].shape
    lowrank = both // 2
    factor = clip_factor(grads)
    me = lax.axis_index("tensor")
    for half in range(2):
        mean_ref, power_ref = state[half], state[2 + half]
        rows = slice(half * lowrank, (half + 1) * lowrank)
        loads[half].wait()
        loads[2 + half].wait()
        for k in range(parts):
            columns = pl.ds(pl.multiple_of((me ^ k) * width, width), width)
            clipped = grads[k][rows, :] * factor
            mean = beta_one * mean_ref[0, :, columns] + (1.0 - beta_one) * clipped
            power = beta_two * power_ref[0, :, columns] + (1.0 - beta_two) * clipped * clipped
            mean_ref[0, :, columns] = mean
            power_ref[0, :, columns] = power
            outs[k][rows, :] = (mean * (learn_rate / correct_one)) / (
                jnp.sqrt(power * (1.0 / correct_two)) + adam_eps
            )
        stores[half].start()
        stores[2 + half].start()
    for store in stores:
        store.wait()


def pack_kernel(*refs):
    for i, ref in enumerate(refs[:-1]):
        refs[-1][i] = ref[...]


def update_kernel(groups, slot_ref, down_ref, up_ref, *refs):
    down_out, up_out = refs[-2:]
    lowrank = down_ref.shape[1]
    me, core, cores = lax.axis_index("tensor"), lax.axis_index("dp"), lax.axis_size("dp")
    for i, ks in enumerate(groups):
        for j in range(2):
            for n, k in enumerate(ks):
                tenant = slot_ref[(me ^ k) * cores + (core ^ j)]
                block = refs[2 * i + j][n]
                down_out[tenant] = (down_ref[tenant].astype(f32) - block[:lowrank]).astype(bf16)
                up_out[tenant] = (up_ref[tenant].astype(f32) - block[lowrank:]).astype(bf16)


def swap(x, axis, bits):
    size = lax.axis_size(axis)
    return lax.ppermute(x, axis, [(i, i ^ bits) for i in range(size)])


def on_device(
    features,
    cotangent,
    token_tenant,
    owner_device,
    frozen_weight,
    adapter_down,
    adapter_up,
    momentum_down,
    momentum_up,
    variance_down,
    variance_up,
):
    tokens = features.shape[0]
    tenants, lowrank, width = adapter_down.shape
    parts = lax.axis_size("tensor")
    parts_dp = lax.axis_size("dp")
    slot_index = lax.broadcasted_iota(jnp.int32, (tenants, tenants), 0)
    tenant_index = lax.broadcasted_iota(jnp.int32, (tenants, tenants), 1)
    slot_tenant = jnp.sum(jnp.where(owner_device[None, :] == slot_index, tenant_index, 0), axis=1)
    bits = [1 << i for i in range(parts.bit_length() - 1)]
    block = jax.ShapeDtypeStruct((2 * lowrank, width), f32)
    low_both = jax.ShapeDtypeStruct((4 * lowrank, tokens), f32)
    id_rows = jax.ShapeDtypeStruct((8, tokens), f32)
    features, cotangent = in_hbm(features), in_hbm(cotangent)
    frozen_weight = in_hbm(frozen_weight)
    state = [Far(x) for x in (momentum_down, momentum_up, variance_down, variance_up)]

    rank_part, rows, ids = call(
        functools.partial(rank_kernel, tenants, lowrank),
        [
            jax.ShapeDtypeStruct((2 * lowrank + 8, tokens), f32),
            jax.ShapeDtypeStruct((2 * tokens, width), f32),
            id_rows,
        ],
        in_hbm(token_tenant.reshape(1, tokens)), in_hbm(owner_device.reshape(1, tenants)),
        features, cotangent, in_hbm(adapter_down), in_hbm(adapter_up),
        specs=[hbm] * 6,
        scratch=[pltpu.VMEM((1, tokens), jnp.int32), pltpu.VMEM((1, tenants), jnp.int32)]
        + [pltpu.VMEM((tokens, width), bf16)] * 2
        + [pltpu.VMEM(adapter_down.shape, bf16)] * 2
        + [pltpu.SemaphoreType.DMA((6,))],
        name="rank_part",
    )
    cores = [(i, i ^ 1) for i in range(parts_dp)]
    diagonal = [
        (t * parts_dp + i, (t ^ 1) * parts_dp + j) for t in range(parts) for i, j in cores
    ]
    rank_sum, ids_other = call(
        near_kernel, [low_both, id_rows], rank_part, swap(rank_part, "tensor", 1),
        swap(rank_part, "dp", 1), lax.ppermute(rank_part, ("tensor", "dp"), diagonal),
        name="rank_near",
    )
    rows_other = swap(rows, "dp", 1)

    units = width // 128
    cuts = sorted({0, (3 * units + 4) // 8 or 1, (6 * units + 4) // 8, units})
    pieces = [(128 * a, 128 * (b - a)) for a, b in zip(cuts, cuts[1:])]
    frozen = [
        Chunk(rows, frozen_weight, tokens, parts, first, piece) for first, piece in pieces
    ]

    sent = frozen[0].send(rank_sum)
    frozen[0].go()

    done = 1
    while done < len(bits):
        two = bits[done : done + 2]
        steps = two if len(two) == 1 else [two[0], two[1], two[0] ^ two[1]]
        rank_sum = call(
            add_kernel, low_both, rank_sum, *[swap(rank_sum, "tensor", k) for k in steps],
            name="rank_far", after=[sent],
        )
        done += len(two)

    grads = call(
        functools.partial(grad_kernel, parts), [block] * parts,
        rank_sum, ids, ids_other, rows, rows_other, name="gradients",
    )

    order = sorted(range(2, parts), key=lambda k: (-(k // 2), k))
    order.insert(2, 1)

    def exchange(made, beside, arrived, flight):
        for n, k in enumerate(order):
            x = made[k]
            if n >= flight:
                ready = [arrived[j] for j in order[: n - flight + 1]]
                x = release(x, ready[-1:] + beside(n - flight, ready))
            arrived[k] = swap(x, "tensor", k)

    early, late = frozen[:-1], frozen[-1]
    second = early[1:]

    def beside_gradients(n, ready):
        if n == 0:
            return [early[0].keep(*ready)]
        if n == 1:
            return [chunk.send(*ready) for chunk in second]
        if n == 2:
            sent = early[0].merge(*ready)
            for chunk in second:
                chunk.go(sent, got[1])
            return [sent]
        return []

    got = {0: grads[0]}
    exchange(grads, beside_gradients, got, 4)
    own_grads = [got[k] for k in range(parts)]
    made = call(
        functools.partial(change_kernel, parts),
        [block] * parts + [pltpu.HBM(momentum_down.shape, f32)] * 4, *own_grads,
        *[in_hbm(x.array) for x in state],
        specs=[vmem] * parts + [hbm] * 4, name="change", stage=False,
        scratch=[pltpu.VMEM(momentum_down.shape, f32)] * 4 + [pltpu.SemaphoreType.DMA((8,))],
    )
    change, (mean_down, mean_up, power_down, power_up) = made[:parts], made[parts:]

    def beside_changes(n, ready):
        if n == 0:
            return [chunk.keep(*ready) for chunk in second] + [late.send(*ready)]
        if n == 1:
            late.go(back[1], *[chunk.got for chunk in second])
            return []
        if n == 2:
            mine = [chunk.merge(*ready) for chunk in second]
            while early[0].merges:
                mine.append(early[0].merge(*mine))
            return mine + [late.keep(*mine)]
        return []

    back = {0: change[0]}
    exchange(change, beside_changes, back, 4)
    last = back[order[-2]]
    for chunk in second:
        while chunk.merges:
            last = chunk.merge(last)
    late.merge(last, early[0].got, *[back[k] for k in order[3:]])
    while late.merges:
        late.merge(*[chunk.got for chunk in second])
    packed = call(
        pack_kernel, jax.ShapeDtypeStruct((parts, 2 * lowrank, width), f32),
        *[back[k] for k in range(parts)], name="pack", after=[in_hbm(late.out)],
    )
    sides = [packed, swap(packed, "dp", 1)]
    updated_down, updated_up = call(
        functools.partial(update_kernel, [range(parts)]),
        [pltpu.HBM(adapter_down.shape, bf16)] * 2,
        slot_tenant, Far(adapter_down), Far(adapter_up), *sides,
        specs=[smem] + [vmem] * 4,
        name="update",
    )
    projected = call(
        functools.partial(project_kernel, pieces, tenants),
        pltpu.HBM((tokens, width), bf16),
        ids, rank_sum, Far(adapter_up), *[x for chunk in frozen for x in (Far(chunk.hold), chunk.got)],
        name="project", after=[in_hbm(updated_down)],
    )
    return (projected, updated_down, updated_up, mean_down, mean_up, power_down, power_up)


def solution(mesh):
    in_specs = (
        P(("group", "dp"), "tensor"),
        P(("group", "dp"), "tensor"),
        P(("group", "dp")),
        P("group"),
        P("tensor", None),
        P("group", None, "tensor"),
        P("group", None, "tensor"),
        P(("group", "tensor", "dp"), None, None),
        P(("group", "tensor", "dp"), None, None),
        P(("group", "tensor", "dp"), None, None),
        P(("group", "tensor", "dp"), None, None),
    )
    out_specs = (
        P(("group", "dp"), "tensor"),
        P("group", None, "tensor"),
        P("group", None, "tensor"),
        P(("group", "tensor", "dp"), None, None),
        P(("group", "tensor", "dp"), None, None),
        P(("group", "tensor", "dp"), None, None),
        P(("group", "tensor", "dp"), None, None),
    )
    return jax.shard_map(
        on_device, mesh=mesh, in_specs=in_specs, out_specs=out_specs, check_vma=False
    )
```
